32 devices in a mesh: box: 4 (over x, core), grp: 8 (over z, y).
Axes of the slice: x: 2, y: 2, z: 4, core: 2. Of those that a mesh axis runs over, the one named last changes fastest.
Arguments:
- old_phi: float32 [4, 128, 32, 1024], P('box', 'grp'), may hold values from -6 to 6
- old_rhs: float32 [4, 128, 32, 1024], P('box', 'grp'), may hold values from -12 to 12
- old_beta: float32 [4, 128, 32, 1024], P('box', 'grp'), may hold values from 0.25 to 4
- coarse_field: float32 [4, 128, 16, 256], P('box', 'grp'), may hold values from -6 to 6
- old_pos: int32 [128], P('grp'), may hold values from 0 to 127, each once
- refined: int32 [128], P('grp'), may hold values 0 or 1
- new_owner: int32 [128, 1], P('grp'), may hold values from 0 to 7; in each aligned block of 16 rows (0 to 15, 16 to 31, ...) at most 2 rows name the same one
Outputs:
- smoothed: float32 [4, 128, 32, 1024], P('box', 'grp')
The draws below stay inside these ranges and needn't reach their ends.
Inputs may be any that keep to these rules, and one draw needn't show every extreme that they name: `old_pos`: a permutation of the positions of one slab. `new_owner`: in each device's aligned block of 16 slots no owner is named more than 2 times, a bound that some block reaches.
All inputs are finite; a program needn't handle non-finite values. No bound on the sum of `refined` on one device may be relied on, other than what follows from the above.
Results may differ from the reference program's by a relative error of at most 0.000082.
Values sent between devices are 32-bit elements; how exact they have to be, the bound alone decides.
A program may use at most 256 MiB of HBM per device.

```python
import math
import jax
import jax.numpy as jnp
import numpy as np

EDGE = 32
SLOT_DEV = 16
CAP = 2
SWEEPS = 1
SLABS = 4
SLOTS = 128
RECV = 16
N_GRP = 8


def place_ends(array, key, least, top_value):
    shape = array.shape
    spot = [jax.random.randint(jax.random.fold_in(key, axis), (), 0, shape[axis]) for axis in range(len(shape))]
    array = array.at[tuple(spot)].set(least)
    longest = shape.index(max(shape))
    spot[longest] = (spot[longest] + 1) % shape[longest]
    return array.at[tuple(spot)].set(top_value)


def steps_of(own_key, dims, split, smallest, high):
    loudness, own = 1.0, jax.random.fold_in(own_key, 6)
    for dim, parts in split:
        heights = jnp.exp(jax.random.uniform(jax.random.fold_in(own, dim), (parts,), jnp.float32, smallest / len(split), high / len(split)))
        loudness = loudness * jnp.repeat(heights, dims[dim] // parts).reshape([-1 if axis == dim else 1 for axis in range(len(dims))])
    return loudness


def deal_out(key, own, number, rows, number_of, top, bound, slope):
    ranking = jax.random.permutation(key, number_of)
    packed, ordinary = shares(number_of, rows * top, bound, slope, True), shares(number_of, rows * top, bound, slope, False)
    places = jnp.arange(number_of)

    def named(lengths, rotation):
        used = int((lengths > 0).sum())
        fixed = max(1, used // 4)
        passed = fixed + (places - fixed + rotation * (used - fixed)) % max(1, number_of - fixed)
        return jnp.zeros((number_of,), jnp.int32).at[ranking[jnp.where(places < fixed, places, passed)]].set(jnp.asarray(lengths, jnp.int32))

    lengths = jnp.where(number % 4 == 0, named(packed, number // 4), named(ordinary, number - number // 4 - 1))
    mixed = jax.random.permutation(jax.random.fold_in(own, 3), number_of)
    giver, sink = mixed[0:number_of // 2 * 2:2], mixed[1:number_of // 2 * 2:2]
    room = jnp.minimum(lengths[giver] - 1, bound - lengths[sink]) // 2
    room = jnp.where((giver == ranking[0]) | (sink == ranking[0]) | (lengths[sink] == 0), 0, jnp.maximum(room, 0))
    passed = jax.random.randint(jax.random.fold_in(own, 4), (number_of // 2,), 0, 1 << 20) % (room + 1)
    lengths = lengths.at[giver].add(-passed).at[sink].add(passed)
    members = jnp.searchsorted(jnp.cumsum(lengths), jnp.arange(rows * top), side="right").astype(jnp.int32)
    table = members.reshape(top, rows).T
    table = table[jax.random.permutation(jax.random.fold_in(own, 1), rows)]
    rotation = jax.random.randint(jax.random.fold_in(own, 2), (rows, 1), 0, top)
    return jnp.take_along_axis(table, (jnp.arange(top)[None, :] + rotation) % top, axis=1)


def shares(count, total, limit, slope, full):
    portions = [(1 << 20) // math.isqrt(rank ** slope) + 1 for rank in range(1, count + 1)]
    largest = limit if full else min(limit, max(-(-total // count), total * portions[0] // sum(portions)))
    least = 1 if total - largest >= count - 1 else 0
    counts, rest = [largest] + [least] * (count - 1), total - largest - least * (count - 1)
    while rest > 0:
        candidates = [i for i in range(1, count) if counts[i] < largest] or [i for i in range(1, count) if counts[i] < limit]
        whole, left = sum([portions[i] for i in candidates]), rest
        for i in candidates:
            extra = min(limit - counts[i], max(1, left * portions[i] // whole), rest)
            counts[i] = counts[i] + extra
            rest = rest - extra
    return np.array(counts)


def centred(own_key, shape, scale, reach, cuts=(), kind=jnp.bfloat16):
    result = jax.random.normal(own_key, shape, jnp.float32) * scale
    if len(cuts) > 0:
        result = steps_of(own_key, shape, cuts, -0.22, 0.18) * result
    return jnp.clip(result, min=-reach, max=reach).astype(kind)


def setup_inputs(seed: int = 0) -> dict:
    splits = jax.random.split(jax.random.key(seed), 8)
    old_phi = centred(splits[0], (SLABS, SLOTS, EDGE, EDGE * EDGE), 1.0, 6.0, ((0, 4), (1, 8)), jnp.float32)
    old_rhs = centred(splits[1], (SLABS, SLOTS, EDGE, EDGE * EDGE), 2.0, 12.0, ((0, 4), (1, 8)), jnp.float32)
    old_beta = jnp.clip(jnp.exp(math.log(4.0) - 2.7725887 * jax.random.uniform(splits[2], (SLABS, SLOTS, EDGE, EDGE * EDGE), jnp.float32) ** steps_of(splits[2], (SLABS, SLOTS, EDGE, EDGE * EDGE), ((0, 4), (1, 8)), -0.2, 0.2)), 0.25, 4.0)
    coarse_field = centred(splits[3], (SLABS, SLOTS, EDGE // 2, EDGE * EDGE // 4), 1.0, 6.0, ((0, 4), (1, 8)), jnp.float32)
    old_pos = jax.random.permutation(splits[4], SLOTS).astype(jnp.int32)
    refined = place_ends((jax.random.randint(splits[5], (SLOTS,), 0, 7) < 6).astype(jnp.int32), jax.random.fold_in(splits[5], 1), 0, 1)
    new_owner_keys = jax.random.split(jax.random.fold_in(splits[6], 1), SLOTS // SLOT_DEV)
    new_owner_turns = jax.random.permutation(jax.random.fold_in(splits[6], 3), SLOTS // SLOT_DEV)
    new_owner = jax.vmap(lambda own, number: deal_out(jax.random.fold_in(splits[6], 2), own, number, SLOT_DEV, N_GRP, 1, CAP, 1))(new_owner_keys, new_owner_turns).reshape((SLOTS, 1))
    return {"old_phi": old_phi, "old_rhs": old_rhs, "old_beta": old_beta, "coarse_field": coarse_field, "old_pos": old_pos, "refined": refined, "new_owner": new_owner}


def to_grid(per_pos):
    lead = per_pos.shape[0]
    cube = per_pos.reshape(lead, N_GRP, SLOT_DEV, EDGE, EDGE, EDGE)
    return cube.transpose(0, 3, 1, 4, 2, 5).reshape(lead * EDGE, N_GRP * EDGE, SLOT_DEV * EDGE)


def from_grid(grid):
    cube = grid.reshape(SLABS, EDGE, N_GRP, EDGE, SLOT_DEV, EDGE)
    return cube.transpose(0, 2, 4, 1, 3, 5).reshape(SLABS, SLOTS, EDGE, EDGE * EDGE)


def neighbours(padded):
    return [padded[:-2, 1:-1, 1:-1], padded[2:, 1:-1, 1:-1], padded[1:-1, :-2, 1:-1],
            padded[1:-1, 2:, 1:-1], padded[1:-1, 1:-1, :-2], padded[1:-1, 1:-1, 2:]]


def reference(old_phi, old_rhs, old_beta, coarse_field, old_pos, refined, new_owner):
    owner = new_owner[:, 0]
    half = EDGE // 2

    def by_position(field):
        return jnp.zeros_like(field).at[:, old_pos].set(field)

    cube = coarse_field.reshape(SLABS, SLOTS, half, 1, half, 1, half, 1)
    upsampled = jnp.broadcast_to(cube, (SLABS, SLOTS, half, 2, half, 2, half, 2)).reshape(SLABS, SLOTS, EDGE, EDGE * EDGE)
    fine_mask = (refined > 0)[None, :, None, None]
    phi = to_grid(jnp.where(fine_mask, by_position(old_phi), upsampled))
    rhs = to_grid(by_position(old_rhs))
    beta = to_grid(jnp.where(fine_mask, by_position(old_beta), 1.0))
    mask = to_grid(jnp.broadcast_to(fine_mask, (SLABS, SLOTS, EDGE, EDGE * EDGE)))
    size_x, size_y, size_z = phi.shape
    parity = (jnp.arange(size_x, dtype=jnp.int32)[:, None, None] + jnp.arange(size_y, dtype=jnp.int32)[None, :, None]
              + jnp.arange(size_z, dtype=jnp.int32)[None, None, :]) % 2
    beta_pad = jnp.pad(beta, 1)
    mask_pad = jnp.pad(mask, 1)
    for sweep in range(SWEEPS):
        for colour in range(2):
            phi_pad = jnp.pad(phi, 1)
            accum = rhs
            total = jnp.zeros_like(phi)
            for near_phi, near_beta, near_mask in zip(neighbours(phi_pad), neighbours(beta_pad), neighbours(mask_pad)):
                other = jnp.where(near_mask, near_beta, beta)
                weight = 2.0 * beta * other / (beta + other)
                accum = accum + weight * near_phi
                total = total + weight
            phi = jnp.where(mask & (parity == colour), accum / total, phi)
    final = from_grid(phi)
    owner_hot = (owner[:, None] == jnp.arange(N_GRP, dtype=jnp.int32)[None, :]).astype(jnp.int32)
    blocks = owner_hot.reshape(N_GRP, SLOT_DEV, N_GRP)
    before = jnp.cumsum(blocks, axis=1, dtype=jnp.int32) - blocks
    rank = jnp.sum(before * blocks, axis=2, dtype=jnp.int32).reshape(SLOTS)
    source = jnp.arange(SLOTS, dtype=jnp.int32) // SLOT_DEV
    target = owner * RECV + source * CAP + rank
    slot_live = (refined[old_pos] > 0)[None, :, None, None]
    values = jnp.where(slot_live, final[:, old_pos], 0.0)
    return jnp.zeros((SLABS, N_GRP * RECV, EDGE, EDGE * EDGE), phi.dtype).at[:, target].set(values)
```

```python
import functools

import jax
import jax.numpy as jnp
import numpy as np
from jax import lax
from jax.experimental import pallas as pl
from jax.experimental.pallas import tpu as pltpu
from jax.sharding import PartitionSpec as P

CAP = 2
LANES = 128
PHI, BETA, COARSE, META, ROWS = 0, 32, 64, 80, 88
OUTSIDE = -(1 << 20)
STEPS = ((-1, 0), (1, 0), (0, -1), (0, 1))
HIGHEST = lax.Precision.HIGHEST


def turn(x, shift, axis=1):
    shift = shift % x.shape[axis]
    return x if shift == 0 else pltpu.roll(x, shift, axis)


def lane_of(shape):
    return lax.broadcasted_iota(jnp.int32, shape, 1)


def groups_of(x):
    return [x[:, LANES * g : LANES * (g + 1)] for g in range(x.shape[1] // LANES)]


def faces(parts):
    lane = lane_of(parts[0].shape)
    m, a = lane % 32, lane // 32
    tile = jnp.zeros_like(parts[0])
    for g, part in enumerate(parts):
        tile = jnp.where(m == g, turn(part, g), tile)
        tile = jnp.where(m == 16 + g, turn(part, g - 15), tile)
    for k in range(4):
        here = a == k
        tile = jnp.where(here & (m >= 8) & (m < 16), turn(parts[0], 24 * k + 8), tile)
        tile = jnp.where(here & (m >= 24), turn(parts[-1], 24 * k - 72), tile)
    return tile


def spread(tile):
    lane = lane_of(tile.shape)
    m = lane % 32
    along_z = [jnp.where(m == 31, turn(tile, 15 - g), turn(tile, -g)) for g in range(8)]
    low = turn(tile, -8)
    high = turn(tile, 72)
    for a in range(1, 4):
        low = jnp.where(lane // 8 == a, turn(tile, -24 * a - 8), low)
        high = jnp.where((lane - 96) // 8 == a, turn(tile, 72 - 24 * a), high)
    return along_z, low, high


def swapped(tiles):
    m = lane_of(tiles[0].shape) % 32
    pick = jnp.where(m < 8, tiles[3], jnp.where(m < 16, tiles[1], jnp.where(m < 24, tiles[2], tiles[0])))
    return jnp.where(m < 16, turn(pick, -16), turn(pick, 16))


def around(parts, ghost, low_x, high_x, g):
    along_z, low_y, high_y = ghost
    x = parts[g]
    lane = lane_of(x.shape)
    m = lane % 32
    row = lax.broadcasted_iota(jnp.int32, x.shape, 0)
    cut = slice(LANES * g, LANES * (g + 1))
    minus_x = jnp.where(row == 0, low_x[:, cut], turn(x, 1, 0))
    plus_x = jnp.where(row == x.shape[0] - 1, high_x[:, cut], turn(x, -1, 0))
    if g == 0:
        minus_y = jnp.where(lane < 32, low_y, turn(x, 32))
    else:
        minus_y = turn(jnp.where(lane >= 96, parts[g - 1], x), 32)
    if g == len(parts) - 1:
        plus_y = jnp.where(lane >= 96, high_y, turn(x, -32))
    else:
        plus_y = turn(jnp.where(lane < 32, parts[g + 1], x), -32)
    minus_z = jnp.where(m == 0, along_z[g], turn(x, 1))
    plus_z = jnp.where(m == 31, along_z[g], turn(x, -1))
    return [minus_x, plus_x, minus_y, plus_y, minus_z, plus_z]


def half_sweep(colour, phi, rhs, beta, phi_tile, beta_tile, phi_x, beta_x):
    phis, rhss, betas = groups_of(phi), groups_of(rhs), groups_of(beta)
    phi_ghost, beta_ghost = spread(phi_tile), spread(beta_tile)
    out = []
    for g in range(len(phis)):
        b = betas[g]
        near_b = around(betas, beta_ghost, beta_x[0], beta_x[1], g)
        near_p = around(phis, phi_ghost, phi_x[0], phi_x[1], g)
        lane = lane_of(b.shape)
        row = lax.broadcasted_iota(jnp.int32, b.shape, 0)
        accum, total = 0.5 * rhss[g] / b, jnp.zeros_like(b)
        for other, value in zip(near_b, near_p):
            other = jnp.where(other > 0.0, other, b)
            ratio = other / (b + other)
            accum = accum + ratio * value
            total = total + ratio
        mine = (row + lane // 32 + lane) % 2 == colour
        out.append(jnp.where(mine, accum / total, phis[g]))
    return out


def pack_kernel(count, pos, ref, own, phi, beta, coarse, pick, sent, up, down):
    half = coarse.shape[1]
    wide = jnp.dot(
        coarse[...].reshape(count * half, coarse.shape[2]), pick[...],
        precision=HIGHEST, preferred_element_type=jnp.float32,
    )
    lane = lane_of((8, LANES))
    for q in range(count):
        sent[q, COARSE:META, :] = wide[q * half : (q + 1) * half]
        meta = jnp.where(lane == 0, pos[q], jnp.where(lane == 1, ref[q], own[q]))
        sent[q, META:ROWS, :] = meta.astype(jnp.float32)

    def one(q, carry):
        sent[q, PHI:BETA, :] = faces(groups_of(phi[q]))
        sent[q, BETA:COARSE, :] = faces(groups_of(beta[q]))
        down[q, 0:1, :] = phi[q, 0:1, :]
        down[q, 1:2, :] = beta[q, 0:1, :]
        up[q, 0:1, :] = phi[q, 31:32, :]
        up[q, 1:2, :] = beta[q, 31:32, :]
        return carry

    lax.fori_loop(0, count, one, 0)


def first_kernel(
    count, slots, meta, pos, own, phi, rhs, beta, got, low, high,
    out, tile, up, down, beta_tile, coarse_tile, near, source, holder, filled, wide,
):
    q = pl.program_id(0)
    groups = slots // count

    @pl.when(q == 0)
    def _():
        def place(s, carry):
            holder[meta[s]] = s
            return carry

        lax.fori_loop(0, slots, place, 0)

        def clear(s, carry):
            source[s] = -1
            return carry

        lax.fori_loop(0, groups * CAP, clear, 0)

        def empty(s, carry):
            filled[s] = 0
            return carry

        lax.fori_loop(0, groups, empty, 0)

        def give(s, carry):
            to = own[s]
            rank = filled[to]
            filled[to] = rank + 1
            live = meta[slots + pos[s]] > 0
            source[to * CAP + rank] = jnp.where(live, s, -1)
            return carry

        lax.fori_loop(0, count, give, 0)

    here = pos[q]
    row, col = lax.div(here, count), lax.rem(here, count)
    fine_phi, fine_beta, under = [], [], []
    for k, (dy, dz) in enumerate(STEPS):
        y, z = row + dy, col + dz
        inside = (y >= 0) & (y < groups) & (z >= 0) & (z < count)
        spot = jnp.where(inside, y * count + z, 0)
        fine = inside & (meta[slots + spot] > 0)
        slot = holder[spot]
        near[q * 4 + k] = jnp.where(fine, slot, -1)
        fine_phi.append(jnp.where(fine, got[slot, PHI:BETA, :], 0.0))
        fine_beta.append(jnp.where(fine, got[slot, BETA:COARSE, :], 0.0))
        under.append(jnp.where(inside & jnp.logical_not(fine), got[spot, COARSE:META, :], 0.0))
    narrow = swapped(under)
    half = narrow.shape[0]
    wide[pl.ds(0, half, stride=2), :] = narrow
    wide[pl.ds(1, half, stride=2), :] = narrow
    coarse_ghost = wide[...]
    beta_ghost = swapped(fine_beta)
    coarse_tile[0] = coarse_ghost
    beta_tile[0] = beta_ghost
    parts = half_sweep(
        0, phi[0], rhs[0], beta[0], swapped(fine_phi) + coarse_ghost, beta_ghost,
        (low[0, 0:1, :], high[0, 0:1, :]), (low[0, 1:2, :], high[0, 1:2, :]),
    )
    for g, part in enumerate(parts):
        cut = slice(LANES * g, LANES * (g + 1))
        out[0, :, cut] = part
        down[0, :, cut] = part[0:1]
        up[0, :, cut] = part[31:32]
    tile[0] = faces(parts)


def second_kernel(
    near, source, phi, rhs, beta, got, low, high, low_b, high_b, beta_tile, coarse_tile, out
):
    q = source[pl.program_id(0)]

    @pl.when(q < 0)
    def _():
        out[...] = jnp.zeros_like(out)

    @pl.when(q >= 0)
    def _():
        fine_phi = []
        for k in range(4):
            slot = near[q * 4 + k]
            fine_phi.append(jnp.where(slot >= 0, got[jnp.maximum(slot, 0)], 0.0))
        parts = half_sweep(
            1, phi[0], rhs[0], beta[0], swapped(fine_phi) + coarse_tile[0], beta_tile[0],
            (low[0], high[0]), (low_b[0, 1:2, :], high_b[0, 1:2, :]),
        )
        for g, part in enumerate(parts):
            out[0, :, LANES * g : LANES * (g + 1)] = part


def coarse_pick(half):
    lane = np.arange(LANES)
    m, a = lane % 32, lane // 32
    j = m % 8
    y = np.select([m < 8, m < 16, m < 24], [4 * j + a, 0 * a, 4 * j + a], 2 * half - 1 + 0 * a)
    z = np.select([m < 8, m < 16, m < 24], [0 * a, 8 * a + j, 2 * half - 1 + 0 * a], 8 * a + j)
    cell = (y // 2) * half + z // 2
    return (np.arange(half * half)[:, None] == cell[None, :]).astype(np.float32)


def struct(*shape, dtype=jnp.float32):
    return jax.ShapeDtypeStruct(shape, dtype)


def gathered(x):
    return lax.all_gather(x, "grp", axis=0, tiled=True)


def slab_shift(up, down):
    size = lax.axis_size("box")
    ahead = [(i, i + 1) for i in range(size - 1)]
    back = [(j, i) for i, j in ahead]
    return lax.ppermute(up, "box", ahead), lax.ppermute(down, "box", back)


def shards(old_phi, old_rhs, old_beta, coarse_field, old_pos, refined, new_owner):
    phi, rhs, beta, coarse = old_phi[0], old_rhs[0], old_beta[0], coarse_field[0]
    count, edge, area = phi.shape
    groups = lax.axis_size("grp")
    slots = count * groups
    owner = new_owner[:, 0]
    vmem = pl.BlockSpec(memory_space=pltpu.VMEM)
    smem = pl.BlockSpec(memory_space=pltpu.SMEM)
    params = pltpu.CompilerParams(vmem_limit_bytes=48 * 1024 * 1024)
    sent, up, down = pl.pallas_call(
        functools.partial(pack_kernel, count),
        out_shape=(struct(count, ROWS, LANES), struct(count, 2, area), struct(count, 2, area)),
        in_specs=[smem, smem, smem, vmem, vmem, vmem, vmem],
        out_specs=(vmem, vmem, vmem),
        compiler_params=params,
        name="pack",
    )(old_pos, refined, owner, phi, beta, coarse, jnp.asarray(coarse_pick(edge // 2)))
    got = gathered(sent)
    low, high = slab_shift(up, down)
    meta = got[:, META, 0:3].astype(jnp.int32).T.reshape(3 * slots)

    def own(*shape):
        return pl.BlockSpec((1,) + shape, lambda q, *_: (q, 0, 0))

    def full(*shape):
        return pl.BlockSpec(shape, lambda q, *_: (0, 0, 0))

    box = own(edge, area)
    middle, tile, up2, down2, beta_tile, coarse_tile, near, source = pl.pallas_call(
        functools.partial(first_kernel, count, slots),
        out_shape=(
            struct(count, edge, area), struct(count, edge, LANES), struct(count, 1, area),
            struct(count, 1, area), struct(count, edge, LANES), struct(count, edge, LANES),
            struct(count * 4, dtype=jnp.int32), struct(groups * CAP, dtype=jnp.int32),
        ),
        grid_spec=pltpu.PrefetchScalarGridSpec(
            num_scalar_prefetch=3,
            grid=(count,),
            in_specs=[box, box, box, full(slots, ROWS, LANES), own(2, area), own(2, area)],
            out_specs=[
                box, own(edge, LANES), own(1, area), own(1, area), own(edge, LANES),
                own(edge, LANES), smem, smem,
            ],
            scratch_shapes=[
                pltpu.SMEM((slots,), jnp.int32), pltpu.SMEM((groups,), jnp.int32),
                pltpu.VMEM((edge, LANES), jnp.float32),
            ],
        ),
        compiler_params=params,
        name="colour0",
    )(meta, old_pos, owner, phi, rhs, beta, got, low, high)
    got2 = gathered(tile)
    low2, high2 = slab_shift(up2, down2)

    def at(*shape):
        return pl.BlockSpec(
            (1,) + shape, lambda r, near, source: (jnp.maximum(source[r], 0), 0, 0)
        )

    ordered = pl.pallas_call(
        second_kernel,
        out_shape=struct(groups * CAP, edge, area),
        grid_spec=pltpu.PrefetchScalarGridSpec(
            num_scalar_prefetch=2,
            grid=(groups * CAP,),
            in_specs=[
                at(edge, area), at(edge, area), at(edge, area), full(slots, edge, LANES),
                at(1, area), at(1, area), at(2, area), at(2, area), at(edge, LANES),
                at(edge, LANES),
            ],
            out_specs=[box][0],
        ),
        compiler_params=params,
        name="colour1",
    )(near, source, middle, rhs, beta, got2, low2, high2, low, high, beta_tile, coarse_tile)
    moved = lax.all_to_all(
        ordered.reshape(groups, CAP, edge, area), "grp", split_axis=0, concat_axis=0, tiled=True
    )
    return moved.reshape(groups * CAP, edge, area)[None]


def solution(mesh):
    return jax.shard_map(
        shards,
        mesh=mesh,
        in_specs=(
            P("box", "grp", None, None),
            P("box", "grp", None, None),
            P("box", "grp", None, None),
            P("box", "grp", None, None),
            P("grp"),
            P("grp"),
            P("grp", None),
        ),
        out_specs=P("box", "grp", None, None),
        check_vma=False,
    )
```

```python
import functools

import jax
import jax.numpy as jnp
import numpy as np
from jax import lax
from jax.experimental import pallas as pl
from jax.experimental.pallas import tpu as pltpu
from jax.sharding import PartitionSpec as P

CAP = 2
LANES = 128
FACES, COARSE = 32, 8
ROWS = FACES + COARSE
OUTER = 4
STEPS = ((-1, 0), (1, 0), (0, -1), (0, 1))
HIGHEST = lax.Precision.HIGHEST


def turn(x, shift, axis=1):
    shift = shift % x.shape[axis]
    return x if shift == 0 else pltpu.roll(x, shift, axis)


def lane_of(shape):
    return lax.broadcasted_iota(jnp.int32, shape, 1)


def groups_of(x):
    return [x[:, LANES * g : LANES * (g + 1)] for g in range(x.shape[1] // LANES)]


def faces(parts):
    lane = lane_of(parts[0].shape)
    m, a = lane % 32, lane // 32
    tile = jnp.zeros_like(parts[0])
    for g, part in enumerate(parts):
        tile = jnp.where(m == g, turn(part, g), tile)
        tile = jnp.where(m == 16 + g, turn(part, g - 15), tile)
    for k in range(4):
        here = a == k
        tile = jnp.where(here & (m >= 8) & (m < 16), turn(parts[0], 24 * k + 8), tile)
        tile = jnp.where(here & (m >= 24), turn(parts[-1], 24 * k - 72), tile)
    return tile


def spread(tile):
    lane = lane_of(tile.shape)
    m = lane % 32
    along_z = [jnp.where(m == 31, turn(tile, 15 - g), turn(tile, -g)) for g in range(8)]
    low = turn(tile, -8)
    high = turn(tile, 72)
    for a in range(1, 4):
        low = jnp.where(lane // 8 == a, turn(tile, -24 * a - 8), low)
        high = jnp.where((lane - 96) // 8 == a, turn(tile, 72 - 24 * a), high)
    return along_z, low, high


def swapped(tiles):
    m = lane_of(tiles[0].shape) % 32
    pick = jnp.where(m < 8, tiles[3], jnp.where(m < 16, tiles[1], jnp.where(m < 24, tiles[2], tiles[0])))
    return jnp.where(m < 16, turn(pick, -16), turn(pick, 16))


def around(parts, ghost, low_x, high_x, g):
    along_z, low_y, high_y = ghost
    x = parts[g]
    lane = lane_of(x.shape)
    m = lane % 32
    row = lax.broadcasted_iota(jnp.int32, x.shape, 0)
    cut = slice(LANES * g, LANES * (g + 1))
    minus_x = jnp.where(row == 0, low_x[:, cut], turn(x, 1, 0))
    plus_x = jnp.where(row == x.shape[0] - 1, high_x[:, cut], turn(x, -1, 0))
    if g == 0:
        minus_y = jnp.where(lane < 32, low_y, turn(x, 32))
    else:
        minus_y = turn(jnp.where(lane >= 96, parts[g - 1], x), 32)
    if g == len(parts) - 1:
        plus_y = jnp.where(lane >= 96, high_y, turn(x, -32))
    else:
        plus_y = turn(jnp.where(lane < 32, parts[g + 1], x), -32)
    minus_z = jnp.where(m == 0, along_z[g], turn(x, 1))
    plus_z = jnp.where(m == 31, along_z[g], turn(x, -1))
    return [minus_x, plus_x, minus_y, plus_y, minus_z, plus_z]


def half_sweep(colour, phi, rhs, beta, phi_tile, beta_tile, phi_x, beta_x):
    phis, rhss, betas = groups_of(phi), groups_of(rhs), groups_of(beta)
    phi_ghost, beta_ghost = spread(phi_tile), spread(beta_tile)
    out = []
    for g in range(len(phis)):
        b = betas[g]
        near_b = around(betas, beta_ghost, beta_x[0], beta_x[1], g)
        near_p = around(phis, phi_ghost, phi_x[0], phi_x[1], g)
        lane = lane_of(b.shape)
        row = lax.broadcasted_iota(jnp.int32, b.shape, 0)
        accum, total = 0.5 * rhss[g] / b, jnp.zeros_like(b)
        for other, value in zip(near_b, near_p):
            other = jnp.where(other > 0.0, other, b)
            ratio = other / (b + other)
            accum = accum + ratio * value
            total = total + ratio
        mine = (row + lane // 32 + lane) % 2 == colour
        out.append(jnp.where(mine, accum / total, phis[g]))
    return out


def face_colour(shape):
    lane = lane_of(shape)
    m, a = lane % 32, lane // 32
    row = lax.broadcasted_iota(jnp.int32, shape, 0)
    return (row + jnp.where((m & 8) == 0, a, m) + m // 16) % 2


def paired(x, axis):
    even = lax.broadcasted_iota(jnp.int32, x.shape, axis) % 2 == 0
    return jnp.where(even, turn(x, -1, axis), turn(x, 1, axis))


def mixed(colour, phi, beta):
    return jnp.where(face_colour(phi.shape) == colour, phi, paired(beta, 0))


def mixed_row(colour, first, phi, beta):
    lane = lane_of(phi.shape)
    return jnp.where((first + lane // 32 + lane) % 2 == colour, phi, paired(beta, 1))


def folded(x):
    lane = lane_of((COARSE, LANES))
    odd = jnp.where((lane & 8) == 0, lane // 32, lane) % 2 == 1
    return jnp.where(odd, x[COARSE:], x[:COARSE])


def unfolded(t):
    lane = lane_of(t.shape)
    along_z = (lane & 8) == 0
    odd = jnp.where(along_z, lane // 32, lane) % 2 == 1
    low = jnp.where(odd, jnp.where(along_z, turn(t, 32), turn(t, 1)), t)
    high = jnp.where(odd, t, jnp.where(along_z, turn(t, -32), turn(t, -1)))
    return low, high


def pack_kernel(count, pos, ref, phi, beta, coarse, pick, sent, up, down):
    half = coarse.shape[1]
    wide = jnp.dot(
        coarse[...].reshape(count * half, coarse.shape[2]), pick[...],
        precision=HIGHEST, preferred_element_type=jnp.float32,
    )
    lane = lane_of((8, LANES))
    row = lax.broadcasted_iota(jnp.int32, (8, LANES), 0)
    meta = jnp.zeros((8, LANES), jnp.int32)
    for q in range(count):
        sent[q * ROWS + FACES : (q + 1) * ROWS, :] = folded(wide[q * half : (q + 1) * half])
        meta = jnp.where((lane == q) & (row == 0), pos[q], meta)
        meta = jnp.where((lane == q) & (row == 1), ref[q], meta)
    sent[count * ROWS :, :] = meta.astype(jnp.float32)

    def one(q, carry):
        tile = mixed(1, faces(groups_of(phi[q])), faces(groups_of(beta[q])))
        sent[pl.ds(pl.multiple_of(q * ROWS, 8), FACES), :] = tile
        down[q] = mixed_row(1, 0, phi[q, 0:1, :], beta[q, 0:1, :])
        up[q] = mixed_row(1, 1, phi[q, 31:32, :], beta[q, 31:32, :])
        return carry

    lax.fori_loop(0, count, one, 0)


def exchange_kernel(n, slabs, sent, up, down, got, low, high, send, recv, x_send, x_recv, local):
    inner = n // OUTER
    me, slab = lax.axis_index("grp"), lax.axis_index("box")
    z, y = me // inner, me % inner

    def device(to):
        return {"grp": to}

    ends = [(z < OUTER - 1, "grp", me + inner), (z > 0, "grp", me - inner),
            (slab < slabs - 1, "box", slab + 1), (slab > 0, "box", slab - 1)]
    mates = [z * inner + (y + i) % inner for i in range(1, inner)]
    barrier = pltpu.get_barrier_semaphore()
    for there, axis, to in ends:
        @pl.when(there)
        def _(axis=axis, to=to):
            pl.semaphore_signal(barrier, inc=1, device_id={axis: to}, device_id_type=pl.DeviceIdType.MESH)
    for to in mates:
        pl.semaphore_signal(barrier, inc=1, device_id=device(to), device_id_type=pl.DeviceIdType.MESH)
    total = inner - 1
    for there, _, _ in ends:
        total = total + there.astype(jnp.int32)
    pl.semaphore_wait(barrier, total)

    def copy(src, block, lane, to):
        return pltpu.make_async_remote_copy(
            src_ref=src, dst_ref=got.at[block], send_sem=send.at[lane, block],
            recv_sem=recv.at[block], device_id=device(to), device_id_type=pl.DeviceIdType.MESH,
        )

    def beside(block, src):
        for i, to in enumerate(mates):
            copy(src, block, 2 + i, to).start()

    def along_x(src, dst, lane, to):
        return pltpu.make_async_remote_copy(
            src_ref=src, dst_ref=dst, send_sem=x_send.at[lane], recv_sem=x_recv.at[lane],
            device_id={"box": to}, device_id_type=pl.DeviceIdType.MESH,
        )

    pl.when(z < OUTER - 1)(lambda: copy(sent, me, 0, me + inner).start())
    pl.when(z > 0)(lambda: copy(sent, me, 1, me - inner).start())
    beside(me, sent)
    pl.when(slab < slabs - 1)(lambda: along_x(up, low, 0, slab + 1).start())
    pl.when(slab > 0)(lambda: along_x(down, high, 1, slab - 1).start())
    own = pltpu.make_async_copy(sent, got.at[me], local)
    own.start()
    for s in range(1, OUTER):
        @pl.when(z >= s)
        def _(s=s):
            block = me - s * inner
            copy(got.at[block], block, 0, block).wait_recv()
            pl.when(z < OUTER - 1)(lambda: copy(got.at[block], block, 0, me + inner).start())
            beside(block, got.at[block])

        @pl.when(z + s < OUTER)
        def _(s=s):
            block = me + s * inner
            copy(got.at[block], block, 1, block).wait_recv()
            pl.when(z > 0)(lambda: copy(got.at[block], block, 1, me - inner).start())
            beside(block, got.at[block])
    for level in range(OUTER):
        for i, to in enumerate(mates):
            block = level * inner + (y + i + 1) % inner
            copy(got.at[block], block, 2, to).wait_recv()
    own.wait()
    pl.when(slab > 0)(lambda: along_x(up, low, 0, slab - 1).wait_recv())
    pl.when(slab < slabs - 1)(lambda: along_x(down, high, 1, slab + 1).wait_recv())
    for level in range(OUTER):
        block = level * inner + y
        pl.when((z < OUTER - 1) & (level <= z))(lambda: copy(sent, block, 0, me + inner).wait_send())
        pl.when((z > 0) & (level >= z))(lambda: copy(sent, block, 1, me - inner).wait_send())
        for i, to in enumerate(mates):
            copy(sent, block, 2 + i, to).wait_send()
    pl.when(slab < slabs - 1)(lambda: along_x(up, low, 0, slab + 1).wait_send())
    pl.when(slab > 0)(lambda: along_x(down, high, 1, slab - 1).wait_send())


def exchanged(number, sent, up, down):
    n, slabs = lax.axis_size("grp"), lax.axis_size("box")
    anywhere = pl.BlockSpec(memory_space=pl.ANY)
    return pl.pallas_call(
        functools.partial(exchange_kernel, n, slabs),
        out_shape=(struct(n, *sent.shape), struct(*up.shape), struct(*down.shape)),
        in_specs=[anywhere] * 3,
        out_specs=(anywhere,) * 3,
        scratch_shapes=[
            pltpu.SemaphoreType.DMA((1 + n // OUTER, n)), pltpu.SemaphoreType.DMA((n,)),
            pltpu.SemaphoreType.DMA((2,)), pltpu.SemaphoreType.DMA((2,)), pltpu.SemaphoreType.DMA,
        ],
        compiler_params=pltpu.CompilerParams(collective_id=number, has_side_effects=True),
        name="exchange",
    )(sent, up, down)


def halo_rows(low, high):
    slab, slabs = lax.axis_index("box"), lax.axis_size("box")
    below = jnp.where(slab > 0, low, 0.0)
    above = jnp.where(slab < slabs - 1, high, 0.0)
    return (below, above), (paired(below, 1), paired(above, 1))


def first_kernel(
    count, slots, meta, pos, own, phi, rhs, beta, got, low, high,
    out, tile, up, down, coarse_tile, near, source, holder, filled, wide,
):
    q = pl.program_id(0)
    groups = slots // count

    def refined_at(p):
        return meta[(lax.div(p, count) * 2 + 1) * count + lax.rem(p, count)] > 0

    def rows(s, first, length):
        start = pl.multiple_of(lax.rem(s, count) * ROWS + first, 8)
        return got[lax.div(s, count), pl.ds(start, length), :]

    @pl.when(q == 0)
    def _():
        def place(s, carry):
            holder[meta[lax.div(s, count) * 2 * count + lax.rem(s, count)]] = s
            return carry

        lax.fori_loop(0, slots, place, 0)

        def clear(s, carry):
            source[s] = -1
            return carry

        lax.fori_loop(0, groups * CAP, clear, 0)

        def empty(s, carry):
            filled[s] = 0
            return carry

        lax.fori_loop(0, groups, empty, 0)

        def give(s, carry):
            to = own[s]
            rank = filled[to]
            filled[to] = rank + 1
            live = refined_at(pos[s])
            source[to * CAP + rank] = jnp.where(live, s, -1)
            return carry

        lax.fori_loop(0, count, give, 0)

    here = pos[q]
    row, col = lax.div(here, count), lax.rem(here, count)
    fine_tiles, under = [], []
    for k, (dy, dz) in enumerate(STEPS):
        y, z = row + dy, col + dz
        inside = (y >= 0) & (y < groups) & (z >= 0) & (z < count)
        spot = jnp.where(inside, y * count + z, 0)
        fine = inside & refined_at(spot)
        slot = holder[spot]
        near[q * 4 + k] = jnp.where(fine, slot, -1)
        fine_tiles.append(jnp.where(fine, rows(slot, 0, FACES), 0.0))
        under.append(jnp.where(inside & jnp.logical_not(fine), rows(spot, FACES, COARSE), 0.0))
    for i, narrow in enumerate(unfolded(swapped(under))):
        for odd in range(2):
            wide[pl.ds(2 * COARSE * i + odd, COARSE, stride=2), :] = narrow
    coarse_ghost = wide[...]
    coarse_tile[0] = coarse_ghost
    ghost = swapped(fine_tiles)
    phi_x, beta_x = halo_rows(low[0], high[0])
    parts = half_sweep(
        0, phi[0], rhs[0], beta[0], ghost + coarse_ghost, paired(ghost, 0), phi_x, beta_x
    )
    for g, part in enumerate(parts):
        cut = slice(LANES * g, LANES * (g + 1))
        out[0, :, cut] = part
        down[0, :, cut] = mixed_row(0, 0, part[0:1], beta[0, 0:1, cut])
        up[0, :, cut] = mixed_row(0, 1, part[31:32], beta[0, 31:32, cut])
    tile[...] = mixed(0, faces(parts), faces(groups_of(beta[0])))


def second_kernel(
    near, source, phi, rhs, beta, got, low, high, coarse_tile, out
):
    q = source[pl.program_id(0)]

    @pl.when(q < 0)
    def _():
        out[...] = jnp.zeros_like(out)

    @pl.when(q >= 0)
    def _():
        tiles = []
        for k in range(4):
            slot = near[q * 4 + k]
            tiles.append(jnp.where(slot >= 0, got[jnp.maximum(slot, 0)], 0.0))
        ghost = swapped(tiles)
        phi_x, beta_x = halo_rows(low[0], high[0])
        parts = half_sweep(
            1, phi[0], rhs[0], beta[0], ghost + coarse_tile[0], paired(ghost, 0), phi_x, beta_x
        )
        for g, part in enumerate(parts):
            out[0, :, LANES * g : LANES * (g + 1)] = part


def coarse_pick(half):
    lane = np.arange(LANES)
    m, a = lane % 32, lane // 32
    j = m % 8
    y = np.select([m < 8, m < 16, m < 24], [4 * j + a, 0 * a, 4 * j + a], 2 * half - 1 + 0 * a)
    z = np.select([m < 8, m < 16, m < 24], [0 * a, 8 * a + j, 2 * half - 1 + 0 * a], 8 * a + j)
    cell = (y // 2) * half + z // 2
    return (np.arange(half * half)[:, None] == cell[None, :]).astype(np.float32)


def struct(*shape, dtype=jnp.float32):
    return jax.ShapeDtypeStruct(shape, dtype)


def shards(old_phi, old_rhs, old_beta, coarse_field, old_pos, refined, new_owner):
    phi, rhs, beta, coarse = old_phi[0], old_rhs[0], old_beta[0], coarse_field[0]
    count, edge, area = phi.shape
    groups = lax.axis_size("grp")
    slots = count * groups
    owner = new_owner[:, 0]
    vmem = pl.BlockSpec(memory_space=pltpu.VMEM)
    smem = pl.BlockSpec(memory_space=pltpu.SMEM)
    params = pltpu.CompilerParams(vmem_limit_bytes=48 * 1024 * 1024)
    sent, up, down = pl.pallas_call(
        functools.partial(pack_kernel, count),
        out_shape=(struct(count * ROWS + 8, LANES), struct(count, 1, area), struct(count, 1, area)),
        in_specs=[smem, smem, vmem, vmem, vmem, vmem],
        out_specs=(vmem, vmem, vmem),
        compiler_params=params,
        name="pack",
    )(old_pos, refined, phi, beta, coarse, jnp.asarray(coarse_pick(edge // 2)))
    got, low, high = exchanged(0, sent, up, down)
    meta = got[:, count * ROWS : count * ROWS + 2, :count].astype(jnp.int32).reshape(2 * slots)

    def own(*shape):
        return pl.BlockSpec((1,) + shape, lambda q, *_: (q, 0, 0))

    def full(*shape):
        return pl.BlockSpec(shape, lambda q, *_: (0, 0, 0))

    box = own(edge, area)
    middle, tile, up2, down2, coarse_tile, near, source = pl.pallas_call(
        functools.partial(first_kernel, count, slots),
        out_shape=(
            struct(count, edge, area), struct(count * edge, LANES), struct(count, 1, area),
            struct(count, 1, area), struct(count, edge, LANES),
            struct(count * 4, dtype=jnp.int32), struct(groups * CAP, dtype=jnp.int32),
        ),
        grid_spec=pltpu.PrefetchScalarGridSpec(
            num_scalar_prefetch=3,
            grid=(count,),
            in_specs=[box, box, box, full(groups, count * ROWS + 8, LANES), own(1, area), own(1, area)],
            out_specs=[
                box, pl.BlockSpec((edge, LANES), lambda q, *_: (q, 0)), own(1, area), own(1, area),
                own(edge, LANES), smem, smem,
            ],
            scratch_shapes=[
                pltpu.SMEM((slots,), jnp.int32), pltpu.SMEM((groups,), jnp.int32),
                pltpu.VMEM((edge, LANES), jnp.float32),
            ],
        ),
        compiler_params=params,
        name="colour0",
    )(meta, old_pos, owner, phi, rhs, beta, got, low, high)
    got2, low2, high2 = exchanged(1, tile, up2, down2)

    def at(*shape):
        return pl.BlockSpec(
            (1,) + shape, lambda r, near, source: (jnp.maximum(source[r], 0), 0, 0)
        )

    ordered = pl.pallas_call(
        second_kernel,
        out_shape=struct(groups * CAP, edge, area),
        grid_spec=pltpu.PrefetchScalarGridSpec(
            num_scalar_prefetch=2,
            grid=(groups * CAP,),
            in_specs=[
                at(edge, area), at(edge, area), at(edge, area), full(slots, edge, LANES),
                at(1, area), at(1, area), at(edge, LANES),
            ],
            out_specs=box,
        ),
        compiler_params=params,
        name="colour1",
    )(near, source, middle, rhs, beta, got2.reshape(slots, edge, LANES), low2, high2, coarse_tile)
    moved = lax.all_to_all(
        ordered.reshape(groups, CAP, edge, area), "grp", split_axis=0, concat_axis=0, tiled=True
    )
    return moved.reshape(groups * CAP, edge, area)[None]


def solution(mesh):
    return jax.shard_map(
        shards,
        mesh=mesh,
        in_specs=(
            P("box", "grp", None, None),
            P("box", "grp", None, None),
            P("box", "grp", None, None),
            P("box", "grp", None, None),
            P("grp"),
            P("grp"),
            P("grp", None),
        ),
        out_specs=P("box", "grp", None, None),
        check_vma=False,
    )
```

```python
import functools

import jax
import jax.numpy as jnp
import numpy as np
from jax import lax
from jax.experimental import pallas as pl
from jax.experimental.pallas import tpu as pltpu
from jax.sharding import PartitionSpec as P

CAP = 2
LANES = 128
FACES, COARSE = 32, 8
ROWS = FACES + COARSE
OUTER = 4
VMEM_BYTES = 60 * 1024 * 1024
STEPS = ((-1, 0), (1, 0), (0, -1), (0, 1))
HIGHEST = lax.Precision.HIGHEST


def turn(x, shift, axis=1):
    shift = shift % x.shape[axis]
    return x if shift == 0 else pltpu.roll(x, shift, axis)


def lane_of(shape):
    return lax.broadcasted_iota(jnp.int32, shape, 1)


def groups_of(x):
    return [x[:, LANES * g : LANES * (g + 1)] for g in range(x.shape[1] // LANES)]


def faces(parts):
    lane = lane_of(parts[0].shape)
    m, a = lane % 32, lane // 32
    tile = jnp.zeros_like(parts[0])
    for g, part in enumerate(parts):
        tile = jnp.where(m == g, turn(part, g), tile)
        tile = jnp.where(m == 16 + g, turn(part, g - 15), tile)
    for k in range(4):
        here = a == k
        tile = jnp.where(here & (m >= 8) & (m < 16), turn(parts[0], 24 * k + 8), tile)
        tile = jnp.where(here & (m >= 24), turn(parts[-1], 24 * k - 72), tile)
    return tile


def spread(tile):
    lane = lane_of(tile.shape)
    m = lane % 32
    along_z = [jnp.where(m == 31, turn(tile, 15 - g), turn(tile, -g)) for g in range(8)]
    low = turn(tile, -8)
    high = turn(tile, 72)
    for a in range(1, 4):
        low = jnp.where(lane // 8 == a, turn(tile, -24 * a - 8), low)
        high = jnp.where((lane - 96) // 8 == a, turn(tile, 72 - 24 * a), high)
    return along_z, low, high


def swapped(tiles):
    m = lane_of(tiles[0].shape) % 32
    pick = jnp.where(m < 8, tiles[3], jnp.where(m < 16, tiles[1], jnp.where(m < 24, tiles[2], tiles[0])))
    return jnp.where(m < 16, turn(pick, -16), turn(pick, 16))


def around(parts, ghost, low_x, high_x, g):
    along_z, low_y, high_y = ghost
    x = parts[g]
    lane = lane_of(x.shape)
    m = lane % 32
    row = lax.broadcasted_iota(jnp.int32, x.shape, 0)
    cut = slice(LANES * g, LANES * (g + 1))
    minus_x = jnp.where(row == 0, low_x[:, cut], turn(x, 1, 0))
    plus_x = jnp.where(row == x.shape[0] - 1, high_x[:, cut], turn(x, -1, 0))
    if g == 0:
        minus_y = jnp.where(lane < 32, low_y, turn(x, 32))
    else:
        minus_y = turn(jnp.where(lane >= 96, parts[g - 1], x), 32)
    if g == len(parts) - 1:
        plus_y = jnp.where(lane >= 96, high_y, turn(x, -32))
    else:
        plus_y = turn(jnp.where(lane < 32, parts[g + 1], x), -32)
    minus_z = jnp.where(m == 0, along_z[g], turn(x, 1))
    plus_z = jnp.where(m == 31, along_z[g], turn(x, -1))
    return [minus_x, plus_x, minus_y, plus_y, minus_z, plus_z]


def half_sweep(colour, phi, rhs, beta, phi_tile, beta_tile, phi_x, beta_x):
    phis, rhss, betas = groups_of(phi), groups_of(rhs), groups_of(beta)
    phi_ghost, beta_ghost = spread(phi_tile), spread(beta_tile)
    out = []
    for g in range(len(phis)):
        b = betas[g]
        near_b = around(betas, beta_ghost, beta_x[0], beta_x[1], g)
        near_p = around(phis, phi_ghost, phi_x[0], phi_x[1], g)
        lane = lane_of(b.shape)
        row = lax.broadcasted_iota(jnp.int32, b.shape, 0)
        accum, total = 0.5 * rhss[g] / b, jnp.zeros_like(b)
        for other, value in zip(near_b, near_p):
            other = jnp.where(other > 0.0, other, b)
            ratio = other / (b + other)
            accum = accum + ratio * value
            total = total + ratio
        mine = (row + lane // 32 + lane) % 2 == colour
        out.append(jnp.where(mine, accum / total, phis[g]))
    return out


def face_colour(shape):
    lane = lane_of(shape)
    m, a = lane % 32, lane // 32
    row = lax.broadcasted_iota(jnp.int32, shape, 0)
    return (row + jnp.where((m & 8) == 0, a, m) + m // 16) % 2


def paired(x, axis):
    even = lax.broadcasted_iota(jnp.int32, x.shape, axis) % 2 == 0
    return jnp.where(even, turn(x, -1, axis), turn(x, 1, axis))


def mixed(colour, phi, beta):
    return jnp.where(face_colour(phi.shape) == colour, phi, paired(beta, 0))


def mixed_row(colour, first, phi, beta):
    lane = lane_of(phi.shape)
    return jnp.where((first + lane // 32 + lane) % 2 == colour, phi, paired(beta, 1))


def folded(x):
    lane = lane_of((COARSE, LANES))
    odd = jnp.where((lane & 8) == 0, lane // 32, lane) % 2 == 1
    return jnp.where(odd, x[COARSE:], x[:COARSE])


def unfolded(t):
    lane = lane_of(t.shape)
    along_z = (lane & 8) == 0
    odd = jnp.where(along_z, lane // 32, lane) % 2 == 1
    low = jnp.where(odd, jnp.where(along_z, turn(t, 32), turn(t, 1)), t)
    high = jnp.where(odd, t, jnp.where(along_z, turn(t, -32), turn(t, -1)))
    return low, high


def pack_kernel(count, pos, ref, phi, beta, coarse, pick, sent, up, down):
    q = pl.program_id(0)
    half = coarse.shape[1]

    @pl.when(q == 0)
    def _():
        wide = jnp.dot(
            coarse[...].reshape(count * half, coarse.shape[2]), pick[...],
            precision=HIGHEST, preferred_element_type=jnp.float32,
        )
        lane = lane_of((8, LANES))
        row = lax.broadcasted_iota(jnp.int32, (8, LANES), 0)
        meta = jnp.zeros((8, LANES), jnp.int32)
        for s in range(count):
            sent[s * ROWS + FACES : (s + 1) * ROWS, :] = folded(wide[s * half : (s + 1) * half])
            meta = jnp.where((lane == s) & (row == 0), pos[s], meta)
            meta = jnp.where((lane == s) & (row == 1), ref[s], meta)
        sent[count * ROWS :, :] = meta.astype(jnp.float32)

    tile = mixed(1, faces(groups_of(phi[0])), faces(groups_of(beta[0])))
    sent[pl.ds(pl.multiple_of(q * ROWS, 8), FACES), :] = tile
    down[0] = mixed_row(1, 0, phi[0, 0:1, :], beta[0, 0:1, :])
    up[0] = mixed_row(1, 1, phi[0, 31:32, :], beta[0, 31:32, :])


def exchange_kernel(n, slabs, sent, up, down, got, low, high, send, recv, x_send, x_recv, local):
    inner = n // OUTER
    me, slab = lax.axis_index("grp"), lax.axis_index("box")
    z, y = me // inner, me % inner

    def device(to):
        return {"grp": to}

    ends = [(z < OUTER - 1, "grp", me + inner), (z > 0, "grp", me - inner),
            (slab < slabs - 1, "box", slab + 1), (slab > 0, "box", slab - 1)]
    mates = [z * inner + (y + i) % inner for i in range(1, inner)]
    barrier = pltpu.get_barrier_semaphore()
    for there, axis, to in ends:
        @pl.when(there)
        def _(axis=axis, to=to):
            pl.semaphore_signal(barrier, inc=1, device_id={axis: to}, device_id_type=pl.DeviceIdType.MESH)
    for to in mates:
        pl.semaphore_signal(barrier, inc=1, device_id=device(to), device_id_type=pl.DeviceIdType.MESH)
    total = inner - 1
    for there, _, _ in ends:
        total = total + there.astype(jnp.int32)
    pl.semaphore_wait(barrier, total)

    def copy(src, block, lane, to):
        return pltpu.make_async_remote_copy(
            src_ref=src, dst_ref=got.at[block], send_sem=send.at[lane, block],
            recv_sem=recv.at[block], device_id=device(to), device_id_type=pl.DeviceIdType.MESH,
        )

    def beside(block, src):
        for i, to in enumerate(mates):
            copy(src, block, 2 + i, to).start()

    def along_x(src, dst, lane, to):
        return pltpu.make_async_remote_copy(
            src_ref=src, dst_ref=dst, send_sem=x_send.at[lane], recv_sem=x_recv.at[lane],
            device_id={"box": to}, device_id_type=pl.DeviceIdType.MESH,
        )

    pl.when(z < OUTER - 1)(lambda: copy(sent, me, 0, me + inner).start())
    pl.when(z > 0)(lambda: copy(sent, me, 1, me - inner).start())
    beside(me, sent)
    pl.when(slab < slabs - 1)(lambda: along_x(up, low, 0, slab + 1).start())
    pl.when(slab > 0)(lambda: along_x(down, high, 1, slab - 1).start())
    own = pltpu.make_async_copy(sent, got.at[me], local)
    own.start()
    for s in range(1, OUTER):
        @pl.when(z >= s)
        def _(s=s):
            block = me - s * inner
            copy(got.at[block], block, 0, block).wait_recv()
            pl.when(z < OUTER - 1)(lambda: copy(got.at[block], block, 0, me + inner).start())
            beside(block, got.at[block])

        @pl.when(z + s < OUTER)
        def _(s=s):
            block = me + s * inner
            copy(got.at[block], block, 1, block).wait_recv()
            pl.when(z > 0)(lambda: copy(got.at[block], block, 1, me - inner).start())
            beside(block, got.at[block])
    for level in range(OUTER):
        for i, to in enumerate(mates):
            block = level * inner + (y + i + 1) % inner
            copy(got.at[block], block, 2, to).wait_recv()
    own.wait()
    pl.when(slab > 0)(lambda: along_x(up, low, 0, slab - 1).wait_recv())
    pl.when(slab < slabs - 1)(lambda: along_x(down, high, 1, slab + 1).wait_recv())
    for level in range(OUTER):
        block = level * inner + y
        pl.when((z < OUTER - 1) & (level <= z))(lambda: copy(sent, block, 0, me + inner).wait_send())
        pl.when((z > 0) & (level >= z))(lambda: copy(sent, block, 1, me - inner).wait_send())
        for i, to in enumerate(mates):
            copy(sent, block, 2 + i, to).wait_send()
    pl.when(slab < slabs - 1)(lambda: along_x(up, low, 0, slab + 1).wait_send())
    pl.when(slab > 0)(lambda: along_x(down, high, 1, slab - 1).wait_send())


def exchanged(number, sent, up, down):
    n, slabs = lax.axis_size("grp"), lax.axis_size("box")
    anywhere = pl.BlockSpec(memory_space=pl.ANY)
    return pl.pallas_call(
        functools.partial(exchange_kernel, n, slabs),
        out_shape=(struct(n, *sent.shape), struct(*up.shape), struct(*down.shape)),
        in_specs=[anywhere] * 3,
        out_specs=(anywhere,) * 3,
        scratch_shapes=[
            pltpu.SemaphoreType.DMA((1 + n // OUTER, n)), pltpu.SemaphoreType.DMA((n,)),
            pltpu.SemaphoreType.DMA((2,)), pltpu.SemaphoreType.DMA((2,)), pltpu.SemaphoreType.DMA,
        ],
        compiler_params=pltpu.CompilerParams(
            collective_id=number, has_side_effects=True, vmem_limit_bytes=VMEM_BYTES
        ),
        name="exchange",
    )(sent, up, down)


def halo_rows(low, high):
    slab, slabs = lax.axis_index("box"), lax.axis_size("box")
    below = jnp.where(slab > 0, low, 0.0)
    above = jnp.where(slab < slabs - 1, high, 0.0)
    return (below, above), (paired(below, 1), paired(above, 1))


def first_kernel(
    count, slots, meta, pos, own, phi, rhs, beta, got, low, high,
    out, tile, up, down, coarse_tile, near, source, holder, filled, wide,
):
    q = pl.program_id(0)
    groups = slots // count

    def refined_at(p):
        return meta[(lax.div(p, count) * 2 + 1) * count + lax.rem(p, count)] > 0

    def rows(s, first, length):
        start = pl.multiple_of(lax.rem(s, count) * ROWS + first, 8)
        return got[lax.div(s, count), pl.ds(start, length), :]

    @pl.when(q == 0)
    def _():
        def place(s, carry):
            holder[meta[lax.div(s, count) * 2 * count + lax.rem(s, count)]] = s
            return carry

        lax.fori_loop(0, slots, place, 0)

        def clear(s, carry):
            source[s] = -1
            return carry

        lax.fori_loop(0, groups * CAP, clear, 0)

        def empty(s, carry):
            filled[s] = 0
            return carry

        lax.fori_loop(0, groups, empty, 0)

        def give(s, carry):
            to = own[s]
            rank = filled[to]
            filled[to] = rank + 1
            live = refined_at(pos[s])
            source[to * CAP + rank] = jnp.where(live, s, -1)
            return carry

        lax.fori_loop(0, count, give, 0)

    here = pos[q]
    row, col = lax.div(here, count), lax.rem(here, count)
    fine_tiles, under = [], []
    for k, (dy, dz) in enumerate(STEPS):
        y, z = row + dy, col + dz
        inside = (y >= 0) & (y < groups) & (z >= 0) & (z < count)
        spot = jnp.where(inside, y * count + z, 0)
        fine = inside & refined_at(spot)
        slot = holder[spot]
        near[q * 4 + k] = jnp.where(fine, slot, -1)
        fine_tiles.append(jnp.where(fine, rows(slot, 0, FACES), 0.0))
        under.append(jnp.where(inside & jnp.logical_not(fine), rows(spot, FACES, COARSE), 0.0))
    for i, narrow in enumerate(unfolded(swapped(under))):
        for odd in range(2):
            wide[pl.ds(2 * COARSE * i + odd, COARSE, stride=2), :] = narrow
    coarse_ghost = wide[...]
    coarse_tile[0] = coarse_ghost
    ghost = swapped(fine_tiles)
    phi_x, beta_x = halo_rows(low[0], high[0])
    parts = half_sweep(
        0, phi[0], rhs[0], beta[0], ghost + coarse_ghost, paired(ghost, 0), phi_x, beta_x
    )
    for g, part in enumerate(parts):
        cut = slice(LANES * g, LANES * (g + 1))
        out[0, :, cut] = part
        down[0, :, cut] = mixed_row(0, 0, part[0:1], beta[0, 0:1, cut])
        up[0, :, cut] = mixed_row(0, 1, part[31:32], beta[0, 31:32, cut])
    tile[...] = mixed(0, faces(parts), faces(groups_of(beta[0])))


def second_kernel(
    near, source, phi, rhs, beta, got, low, high, coarse_tile, out
):
    q = source[pl.program_id(0)]

    @pl.when(q < 0)
    def _():
        out[...] = jnp.zeros_like(out)

    @pl.when(q >= 0)
    def _():
        tiles = []
        for k in range(4):
            slot = near[q * 4 + k]
            tiles.append(jnp.where(slot >= 0, got[jnp.maximum(slot, 0)], 0.0))
        ghost = swapped(tiles)
        phi_x, beta_x = halo_rows(low[0], high[0])
        parts = half_sweep(
            1, phi[0], rhs[0], beta[0], ghost + coarse_tile[0], paired(ghost, 0), phi_x, beta_x
        )
        for g, part in enumerate(parts):
            out[0, :, LANES * g : LANES * (g + 1)] = part


def coarse_pick(half):
    lane = np.arange(LANES)
    m, a = lane % 32, lane // 32
    j = m % 8
    y = np.select([m < 8, m < 16, m < 24], [4 * j + a, 0 * a, 4 * j + a], 2 * half - 1 + 0 * a)
    z = np.select([m < 8, m < 16, m < 24], [0 * a, 8 * a + j, 2 * half - 1 + 0 * a], 8 * a + j)
    cell = (y // 2) * half + z // 2
    return (np.arange(half * half)[:, None] == cell[None, :]).astype(np.float32)


def struct(*shape, dtype=jnp.float32):
    return jax.ShapeDtypeStruct(shape, dtype)


def shards(old_phi, old_rhs, old_beta, coarse_field, old_pos, refined, new_owner):
    phi, rhs, beta, coarse = old_phi[0], old_rhs[0], old_beta[0], coarse_field[0]
    count, edge, area = phi.shape
    groups = lax.axis_size("grp")
    slots = count * groups
    owner = new_owner[:, 0]
    smem = pl.BlockSpec(memory_space=pltpu.SMEM)
    params = pltpu.CompilerParams(vmem_limit_bytes=VMEM_BYTES)
    def own(*shape):
        return pl.BlockSpec((1,) + shape, lambda q, *_: (q, 0, 0))

    def full(*shape):
        return pl.BlockSpec(shape, lambda q, *_: (0, 0, 0))

    box = own(edge, area)
    sent, up, down = pl.pallas_call(
        functools.partial(pack_kernel, count),
        out_shape=(
            struct(count * ROWS + 8, LANES), struct(count, 1, area), struct(count, 1, area)
        ),
        grid_spec=pltpu.PrefetchScalarGridSpec(
            num_scalar_prefetch=2,
            grid=(count,),
            in_specs=[
                box, box, full(*coarse.shape), pl.BlockSpec((area // 4, LANES), lambda q, *_: (0, 0))
            ],
            out_specs=[
                pl.BlockSpec((count * ROWS + 8, LANES), lambda q, *_: (0, 0)), own(1, area),
                own(1, area),
            ],
        ),
        compiler_params=params,
        name="pack",
    )(old_pos, refined, phi, beta, coarse, jnp.asarray(coarse_pick(edge // 2)))
    got, low, high = exchanged(0, sent, up, down)
    meta = got[:, count * ROWS : count * ROWS + 2, :count].astype(jnp.int32).reshape(2 * slots)

    middle, tile, up2, down2, coarse_tile, near, source = pl.pallas_call(
        functools.partial(first_kernel, count, slots),
        out_shape=(
            struct(count, edge, area), struct(count * edge, LANES), struct(count, 1, area),
            struct(count, 1, area), struct(count, edge, LANES),
            struct(count * 4, dtype=jnp.int32), struct(groups * CAP, dtype=jnp.int32),
        ),
        grid_spec=pltpu.PrefetchScalarGridSpec(
            num_scalar_prefetch=3,
            grid=(count,),
            in_specs=[box, box, box, full(groups, count * ROWS + 8, LANES), own(1, area), own(1, area)],
            out_specs=[
                box, pl.BlockSpec((edge, LANES), lambda q, *_: (q, 0)), own(1, area), own(1, area),
                own(edge, LANES), smem, smem,
            ],
            scratch_shapes=[
                pltpu.SMEM((slots,), jnp.int32), pltpu.SMEM((groups,), jnp.int32),
                pltpu.VMEM((edge, LANES), jnp.float32),
            ],
        ),
        compiler_params=params,
        name="colour0",
    )(meta, old_pos, owner, phi, rhs, beta, got, low, high)
    got2, low2, high2 = exchanged(1, tile, up2, down2)

    def at(*shape):
        return pl.BlockSpec(
            (1,) + shape, lambda r, near, source: (jnp.maximum(source[r], 0), 0, 0)
        )

    ordered = pl.pallas_call(
        second_kernel,
        out_shape=struct(groups * CAP, edge, area),
        grid_spec=pltpu.PrefetchScalarGridSpec(
            num_scalar_prefetch=2,
            grid=(groups * CAP,),
            in_specs=[
                at(edge, area), at(edge, area), at(edge, area), full(slots, edge, LANES),
                at(1, area), at(1, area), at(edge, LANES),
            ],
            out_specs=box,
        ),
        compiler_params=params,
        name="colour1",
    )(near, source, middle, rhs, beta, got2.reshape(slots, edge, LANES), low2, high2, coarse_tile)
    moved = lax.all_to_all(
        ordered.reshape(groups, CAP, edge, area), "grp", split_axis=0, concat_axis=0, tiled=True
    )
    return moved.reshape(groups * CAP, edge, area)[None]


def solution(mesh):
    return jax.shard_map(
        shards,
        mesh=mesh,
        in_specs=(
            P("box", "grp", None, None),
            P("box", "grp", None, None),
            P("box", "grp", None, None),
            P("box", "grp", None, None),
            P("grp"),
            P("grp"),
            P("grp", None),
        ),
        out_specs=P("box", "grp", None, None),
        check_vma=False,
    )
```

```python
import functools

import jax
import jax.numpy as jnp
import numpy as np
from jax import lax
from jax.experimental import pallas as pl
from jax.experimental.pallas import tpu as pltpu
from jax.sharding import PartitionSpec as P

CAP = 2
LANES = 128
FACES, COARSE = 32, 8
ROWS = FACES + COARSE
OUTER = 4
VMEM_BYTES = 60 * 1024 * 1024
STEPS = ((-1, 0), (1, 0), (0, -1), (0, 1))
HIGHEST = lax.Precision.HIGHEST


def turn(x, shift, axis=1):
    shift = shift % x.shape[axis]
    return x if shift == 0 else pltpu.roll(x, shift, axis)


def lane_of(shape):
    return lax.broadcasted_iota(jnp.int32, shape, 1)


def groups_of(x):
    return [x[:, LANES * g : LANES * (g + 1)] for g in range(x.shape[1] // LANES)]


def faces(parts):
    lane = lane_of(parts[0].shape)
    m, a = lane % 32, lane // 32
    tile = jnp.zeros_like(parts[0])
    for g, part in enumerate(parts):
        tile = jnp.where(m == g, turn(part, g), tile)
        tile = jnp.where(m == 16 + g, turn(part, g - 15), tile)
    for k in range(4):
        here = a == k
        tile = jnp.where(here & (m >= 8) & (m < 16), turn(parts[0], 24 * k + 8), tile)
        tile = jnp.where(here & (m >= 24), turn(parts[-1], 24 * k - 72), tile)
    return tile


def spread(tile):
    lane = lane_of(tile.shape)
    m = lane % 32
    along_z = [jnp.where(m == 31, turn(tile, 15 - g), turn(tile, -g)) for g in range(8)]
    low = turn(tile, -8)
    high = turn(tile, 72)
    for a in range(1, 4):
        low = jnp.where(lane // 8 == a, turn(tile, -24 * a - 8), low)
        high = jnp.where((lane - 96) // 8 == a, turn(tile, 72 - 24 * a), high)
    return along_z, low, high


def swapped(tiles):
    m = lane_of(tiles[0].shape) % 32
    pick = jnp.where(m < 8, tiles[3], jnp.where(m < 16, tiles[1], jnp.where(m < 24, tiles[2], tiles[0])))
    return jnp.where(m < 16, turn(pick, -16), turn(pick, 16))


def around(parts, ghost, low_x, high_x, g):
    along_z, low_y, high_y = ghost
    x = parts[g]
    lane = lane_of(x.shape)
    m = lane % 32
    row = lax.broadcasted_iota(jnp.int32, x.shape, 0)
    cut = slice(LANES * g, LANES * (g + 1))
    minus_x = jnp.where(row == 0, low_x[:, cut], turn(x, 1, 0))
    plus_x = jnp.where(row == x.shape[0] - 1, high_x[:, cut], turn(x, -1, 0))
    if g == 0:
        minus_y = jnp.where(lane < 32, low_y, turn(x, 32))
    else:
        minus_y = turn(jnp.where(lane >= 96, parts[g - 1], x), 32)
    if g == len(parts) - 1:
        plus_y = jnp.where(lane >= 96, high_y, turn(x, -32))
    else:
        plus_y = turn(jnp.where(lane < 32, parts[g + 1], x), -32)
    minus_z = jnp.where(m == 0, along_z[g], turn(x, 1))
    plus_z = jnp.where(m == 31, along_z[g], turn(x, -1))
    return [minus_x, plus_x, minus_y, plus_y, minus_z, plus_z]


def half_sweep(colour, phi, rhs, beta, phi_tile, beta_tile, phi_x, beta_x):
    phis, rhss, betas = groups_of(phi), groups_of(rhs), groups_of(beta)
    phi_ghost, beta_ghost = spread(phi_tile), spread(beta_tile)
    out = []
    for g in range(len(phis)):
        b = betas[g]
        near_b = around(betas, beta_ghost, beta_x[0], beta_x[1], g)
        near_p = around(phis, phi_ghost, phi_x[0], phi_x[1], g)
        lane = lane_of(b.shape)
        row = lax.broadcasted_iota(jnp.int32, b.shape, 0)
        accum, total = 0.5 * rhss[g] / b, jnp.zeros_like(b)
        for other, value in zip(near_b, near_p):
            other = jnp.where(other > 0.0, other, b)
            ratio = other / (b + other)
            accum = accum + ratio * value
            total = total + ratio
        mine = (row + lane // 32 + lane) % 2 == colour
        out.append(jnp.where(mine, accum / total, phis[g]))
    return out


def face_colour(shape):
    lane = lane_of(shape)
    m, a = lane % 32, lane // 32
    row = lax.broadcasted_iota(jnp.int32, shape, 0)
    return (row + jnp.where((m & 8) == 0, a, m) + m // 16) % 2


def paired(x, axis):
    even = lax.broadcasted_iota(jnp.int32, x.shape, axis) % 2 == 0
    return jnp.where(even, turn(x, -1, axis), turn(x, 1, axis))


def mixed(colour, phi, beta):
    return jnp.where(face_colour(phi.shape) == colour, phi, paired(beta, 0))


def mixed_row(colour, first, phi, beta):
    lane = lane_of(phi.shape)
    return jnp.where((first + lane // 32 + lane) % 2 == colour, phi, paired(beta, 1))


def folded(x):
    lane = lane_of((COARSE, LANES))
    odd = jnp.where((lane & 8) == 0, lane // 32, lane) % 2 == 1
    return jnp.where(odd, x[COARSE:], x[:COARSE])


def unfolded(t):
    lane = lane_of(t.shape)
    along_z = (lane & 8) == 0
    odd = jnp.where(along_z, lane // 32, lane) % 2 == 1
    low = jnp.where(odd, jnp.where(along_z, turn(t, 32), turn(t, 1)), t)
    high = jnp.where(odd, t, jnp.where(along_z, turn(t, -32), turn(t, -1)))
    return low, high


def pack_kernel(count, pos, ref, phi, beta, coarse, pick, sent, up, down):
    q = pl.program_id(0)
    half = coarse.shape[1]

    @pl.when(q == 0)
    def _():
        wide = jnp.dot(
            coarse[...].reshape(count * half, coarse.shape[2]), pick[...],
            precision=HIGHEST, preferred_element_type=jnp.float32,
        )
        lane = lane_of((8, LANES))
        row = lax.broadcasted_iota(jnp.int32, (8, LANES), 0)
        meta = jnp.zeros((8, LANES), jnp.int32)
        for s in range(count):
            sent[s * ROWS + FACES : (s + 1) * ROWS, :] = folded(wide[s * half : (s + 1) * half])
            meta = jnp.where((lane == s) & (row == 0), pos[s], meta)
            meta = jnp.where((lane == s) & (row == 1), ref[s], meta)
        sent[count * ROWS :, :] = meta.astype(jnp.float32)

    tile = mixed(1, faces(groups_of(phi[0])), faces(groups_of(beta[0])))
    sent[pl.ds(pl.multiple_of(q * ROWS, 8), FACES), :] = tile
    down[0] = mixed_row(1, 0, phi[0, 0:1, :], beta[0, 0:1, :])
    up[0] = mixed_row(1, 1, phi[0, 31:32, :], beta[0, 31:32, :])


def exchange_kernel(n, slabs, sent, up, down, got, low, high, send, recv, x_send, x_recv, local):
    inner = n // OUTER
    me, slab = lax.axis_index("grp"), lax.axis_index("box")
    z, y = me // inner, me % inner

    def device(to):
        return {"grp": to}

    ends = [(z < OUTER - 1, "grp", me + inner), (z > 0, "grp", me - inner),
            (slab < slabs - 1, "box", slab + 1), (slab > 0, "box", slab - 1)]
    mates = [z * inner + (y + i) % inner for i in range(1, inner)]
    barrier = pltpu.get_barrier_semaphore()
    for there, axis, to in ends:
        @pl.when(there)
        def _(axis=axis, to=to):
            pl.semaphore_signal(barrier, inc=1, device_id={axis: to}, device_id_type=pl.DeviceIdType.MESH)
    for to in mates:
        pl.semaphore_signal(barrier, inc=1, device_id=device(to), device_id_type=pl.DeviceIdType.MESH)
    total = inner - 1
    for there, _, _ in ends:
        total = total + there.astype(jnp.int32)
    pl.semaphore_wait(barrier, total)

    def copy(src, block, lane, to):
        return pltpu.make_async_remote_copy(
            src_ref=src, dst_ref=got.at[block], send_sem=send.at[lane, block],
            recv_sem=recv.at[block], device_id=device(to), device_id_type=pl.DeviceIdType.MESH,
        )

    def beside(block, src):
        for i, to in enumerate(mates):
            copy(src, block, 2 + i, to).start()

    def along_x(src, dst, lane, to):
        return pltpu.make_async_remote_copy(
            src_ref=src, dst_ref=dst, send_sem=x_send.at[lane], recv_sem=x_recv.at[lane],
            device_id={"box": to}, device_id_type=pl.DeviceIdType.MESH,
        )

    pl.when(z < OUTER - 1)(lambda: copy(sent, me, 0, me + inner).start())
    pl.when(z > 0)(lambda: copy(sent, me, 1, me - inner).start())
    beside(me, sent)
    pl.when(slab < slabs - 1)(lambda: along_x(up, low, 0, slab + 1).start())
    pl.when(slab > 0)(lambda: along_x(down, high, 1, slab - 1).start())
    own = pltpu.make_async_copy(sent, got.at[me], local)
    own.start()
    for s in range(1, OUTER):
        @pl.when(z >= s)
        def _(s=s):
            block = me - s * inner
            copy(got.at[block], block, 0, block).wait_recv()
            pl.when(z < OUTER - 1)(lambda: copy(got.at[block], block, 0, me + inner).start())
            beside(block, got.at[block])

        @pl.when(z + s < OUTER)
        def _(s=s):
            block = me + s * inner
            copy(got.at[block], block, 1, block).wait_recv()
            pl.when(z > 0)(lambda: copy(got.at[block], block, 1, me - inner).start())
            beside(block, got.at[block])
    for level in range(OUTER):
        for i, to in enumerate(mates):
            block = level * inner + (y + i + 1) % inner
            copy(got.at[block], block, 2, to).wait_recv()
    own.wait()
    pl.when(slab > 0)(lambda: along_x(up, low, 0, slab - 1).wait_recv())
    pl.when(slab < slabs - 1)(lambda: along_x(down, high, 1, slab + 1).wait_recv())
    for level in range(OUTER):
        block = level * inner + y
        pl.when((z < OUTER - 1) & (level <= z))(lambda: copy(sent, block, 0, me + inner).wait_send())
        pl.when((z > 0) & (level >= z))(lambda: copy(sent, block, 1, me - inner).wait_send())
        for i, to in enumerate(mates):
            copy(sent, block, 2 + i, to).wait_send()
    pl.when(slab < slabs - 1)(lambda: along_x(up, low, 0, slab + 1).wait_send())
    pl.when(slab > 0)(lambda: along_x(down, high, 1, slab - 1).wait_send())


def exchanged(number, sent, up, down):
    n, slabs = lax.axis_size("grp"), lax.axis_size("box")
    anywhere = pl.BlockSpec(memory_space=pl.ANY)
    return pl.pallas_call(
        functools.partial(exchange_kernel, n, slabs),
        out_shape=(struct(n, *sent.shape), struct(*up.shape), struct(*down.shape)),
        in_specs=[anywhere] * 3,
        out_specs=(anywhere,) * 3,
        scratch_shapes=[
            pltpu.SemaphoreType.DMA((1 + n // OUTER, n)), pltpu.SemaphoreType.DMA((n,)),
            pltpu.SemaphoreType.DMA((2,)), pltpu.SemaphoreType.DMA((2,)), pltpu.SemaphoreType.DMA,
        ],
        compiler_params=pltpu.CompilerParams(
            collective_id=number, has_side_effects=True, vmem_limit_bytes=VMEM_BYTES
        ),
        name="exchange",
    )(sent, up, down)


def halo_rows(low, high):
    slab, slabs = lax.axis_index("box"), lax.axis_size("box")
    below = jnp.where(slab > 0, low, 0.0)
    above = jnp.where(slab < slabs - 1, high, 0.0)
    return (below, above), (paired(below, 1), paired(above, 1))


def first_kernel(
    count, slots, meta, pos, own, phi, rhs, beta, got, low, high,
    out, tile, up, down, coarse_tile, near, source, holder, filled, wide,
):
    q = pl.program_id(0)
    groups = slots // count

    def refined_at(p):
        return meta[(lax.div(p, count) * 2 + 1) * count + lax.rem(p, count)] > 0

    def rows(s, first, length):
        start = pl.multiple_of(lax.rem(s, count) * ROWS + first, 8)
        return got[lax.div(s, count), pl.ds(start, length), :]

    @pl.when(q == 0)
    def _():
        def place(s, carry):
            holder[meta[lax.div(s, count) * 2 * count + lax.rem(s, count)]] = s
            return carry

        lax.fori_loop(0, slots, place, 0)

        def clear(s, carry):
            source[s] = -1
            return carry

        lax.fori_loop(0, groups * CAP, clear, 0)

        def empty(s, carry):
            filled[s] = 0
            return carry

        lax.fori_loop(0, groups, empty, 0)

        def give(s, carry):
            to = own[s]
            rank = filled[to]
            filled[to] = rank + 1
            live = refined_at(pos[s])
            source[to * CAP + rank] = jnp.where(live, s, -1)
            return carry

        lax.fori_loop(0, count, give, 0)

    here = pos[q]
    row, col = lax.div(here, count), lax.rem(here, count)
    fine_tiles, under = [], []
    for k, (dy, dz) in enumerate(STEPS):
        y, z = row + dy, col + dz
        inside = (y >= 0) & (y < groups) & (z >= 0) & (z < count)
        spot = jnp.where(inside, y * count + z, 0)
        fine = inside & refined_at(spot)
        slot = holder[spot]
        near[q * 4 + k] = jnp.where(fine, slot, -1)
        fine_tiles.append(jnp.where(fine, rows(slot, 0, FACES), 0.0))
        under.append(jnp.where(inside & jnp.logical_not(fine), rows(spot, FACES, COARSE), 0.0))
    for i, narrow in enumerate(unfolded(swapped(under))):
        for odd in range(2):
            wide[pl.ds(2 * COARSE * i + odd, COARSE, stride=2), :] = narrow
    coarse_ghost = wide[...]
    coarse_tile[0] = coarse_ghost
    ghost = swapped(fine_tiles)
    phi_x, beta_x = halo_rows(low[0], high[0])
    parts = half_sweep(
        0, phi[0], rhs[0], beta[0], ghost + coarse_ghost, paired(ghost, 0), phi_x, beta_x
    )
    for g, part in enumerate(parts):
        cut = slice(LANES * g, LANES * (g + 1))
        out[0, :, cut] = part
        down[0, :, cut] = mixed_row(0, 0, part[0:1], beta[0, 0:1, cut])
        up[0, :, cut] = mixed_row(0, 1, part[31:32], beta[0, 31:32, cut])
    tile[...] = mixed(0, faces(parts), faces(groups_of(beta[0])))


def deliver_kernel(
    n, near, source, phi, rhs, beta, got, low, high, coarse_tile, moved, ready, send, recv, local
):
    me = lax.axis_index("grp")
    barrier = pltpu.get_barrier_semaphore()
    for i in range(1, n):
        pl.semaphore_signal(
            barrier, inc=1, device_id={"grp": (me + i) % n}, device_id_type=pl.DeviceIdType.MESH
        )
    pl.semaphore_wait(barrier, n - 1)
    side, place = me // (n // 2), me % (n // 2)

    def copy(mine, theirs, to):
        return pltpu.make_async_remote_copy(
            src_ref=ready.at[mine], dst_ref=moved.at[theirs], send_sem=send.at[mine],
            recv_sem=recv.at[theirs], device_id={"grp": to}, device_id_type=pl.DeviceIdType.MESH,
        )

    def solve(mine):
        q = source[mine]
        box = jnp.maximum(q, 0)
        tiles = []
        for k in range(4):
            slot = near[box * 4 + k]
            tiles.append(jnp.where(slot >= 0, got[jnp.maximum(slot, 0)], 0.0))
        ghost = swapped(tiles)
        phi_x, beta_x = halo_rows(low[box], high[box])
        parts = half_sweep(
            1, phi[box], rhs[box], beta[box], ghost + coarse_tile[box], paired(ghost, 0),
            phi_x, beta_x,
        )
        for g, part in enumerate(parts):
            ready[mine, :, LANES * g : LANES * (g + 1)] = jnp.where(q >= 0, part, 0.0)

    def one(t, carry):
        i, c = t // CAP, t % CAP
        far = (1 - side) * (n // 2) + (place + i) % (n // 2)
        close = side * (n // 2) + (place + i + 1) % (n // 2)
        to = jnp.where(i < n // 2, far, close)
        mine = to * CAP + c
        solve(mine)
        pl.when(i < n - 1)(lambda: copy(mine, me * CAP + c, to).start())
        return carry

    lax.fori_loop(0, n * CAP, one, 0)
    own = [
        pltpu.make_async_copy(ready.at[me * CAP + c], moved.at[me * CAP + c], local.at[c])
        for c in range(CAP)
    ]
    for each in own:
        each.start()
    for i in range(1, n):
        other = (me + i) % n
        for c in range(CAP):
            copy(other * CAP + c, other * CAP + c, other).wait()
    for each in own:
        each.wait()


def coarse_pick(half):
    lane = np.arange(LANES)
    m, a = lane % 32, lane // 32
    j = m % 8
    y = np.select([m < 8, m < 16, m < 24], [4 * j + a, 0 * a, 4 * j + a], 2 * half - 1 + 0 * a)
    z = np.select([m < 8, m < 16, m < 24], [0 * a, 8 * a + j, 2 * half - 1 + 0 * a], 8 * a + j)
    cell = (y // 2) * half + z // 2
    return (np.arange(half * half)[:, None] == cell[None, :]).astype(np.float32)


def struct(*shape, dtype=jnp.float32):
    return jax.ShapeDtypeStruct(shape, dtype)


def shards(old_phi, old_rhs, old_beta, coarse_field, old_pos, refined, new_owner):
    phi, rhs, beta, coarse = old_phi[0], old_rhs[0], old_beta[0], coarse_field[0]
    count, edge, area = phi.shape
    groups = lax.axis_size("grp")
    slots = count * groups
    owner = new_owner[:, 0]
    smem = pl.BlockSpec(memory_space=pltpu.SMEM)
    params = pltpu.CompilerParams(vmem_limit_bytes=VMEM_BYTES)
    def own(*shape):
        return pl.BlockSpec((1,) + shape, lambda q, *_: (q, 0, 0))

    def full(*shape):
        return pl.BlockSpec(shape, lambda q, *_: (0, 0, 0))

    box = own(edge, area)
    sent, up, down = pl.pallas_call(
        functools.partial(pack_kernel, count),
        out_shape=(
            struct(count * ROWS + 8, LANES), struct(count, 1, area), struct(count, 1, area)
        ),
        grid_spec=pltpu.PrefetchScalarGridSpec(
            num_scalar_prefetch=2,
            grid=(count,),
            in_specs=[
                box, box, full(*coarse.shape), pl.BlockSpec((area // 4, LANES), lambda q, *_: (0, 0))
            ],
            out_specs=[
                pl.BlockSpec((count * ROWS + 8, LANES), lambda q, *_: (0, 0)), own(1, area),
                own(1, area),
            ],
        ),
        compiler_params=params,
        name="pack",
    )(old_pos, refined, phi, beta, coarse, jnp.asarray(coarse_pick(edge // 2)))
    got, low, high = exchanged(0, sent, up, down)
    meta = got[:, count * ROWS : count * ROWS + 2, :count].astype(jnp.int32).reshape(2 * slots)

    middle, tile, up2, down2, coarse_tile, near, source = pl.pallas_call(
        functools.partial(first_kernel, count, slots),
        out_shape=(
            struct(count, edge, area), struct(count * edge, LANES), struct(count, 1, area),
            struct(count, 1, area), struct(count, edge, LANES),
            struct(count * 4, dtype=jnp.int32), struct(groups * CAP, dtype=jnp.int32),
        ),
        grid_spec=pltpu.PrefetchScalarGridSpec(
            num_scalar_prefetch=3,
            grid=(count,),
            in_specs=[box, box, box, full(groups, count * ROWS + 8, LANES), own(1, area), own(1, area)],
            out_specs=[
                box, pl.BlockSpec((edge, LANES), lambda q, *_: (q, 0)), own(1, area), own(1, area),
                own(edge, LANES), smem, smem,
            ],
            scratch_shapes=[
                pltpu.SMEM((slots,), jnp.int32), pltpu.SMEM((groups,), jnp.int32),
                pltpu.VMEM((edge, LANES), jnp.float32),
            ],
        ),
        compiler_params=params,
        name="colour0",
    )(meta, old_pos, owner, phi, rhs, beta, got, low, high)
    got2, low2, high2 = exchanged(1, tile, up2, down2)

    vmem = pl.BlockSpec(memory_space=pltpu.VMEM)
    moved = pl.pallas_call(
        functools.partial(deliver_kernel, groups),
        out_shape=struct(groups * CAP, edge, area),
        in_specs=[smem, smem] + [vmem] * 7,
        out_specs=pl.BlockSpec(memory_space=pl.ANY),
        scratch_shapes=[
            pltpu.VMEM((groups * CAP, edge, area), jnp.float32),
            pltpu.SemaphoreType.DMA((groups * CAP,)), pltpu.SemaphoreType.DMA((groups * CAP,)),
            pltpu.SemaphoreType.DMA((CAP,)),
        ],
        compiler_params=pltpu.CompilerParams(
            collective_id=2, has_side_effects=True, vmem_limit_bytes=VMEM_BYTES
        ),
        name="deliver",
    )(near, source, middle, rhs, beta, got2.reshape(slots, edge, LANES), low2, high2, coarse_tile)
    return moved[None]


def solution(mesh):
    return jax.shard_map(
        shards,
        mesh=mesh,
        in_specs=(
            P("box", "grp", None, None),
            P("box", "grp", None, None),
            P("box", "grp", None, None),
            P("box", "grp", None, None),
            P("grp"),
            P("grp"),
            P("grp", None),
        ),
        out_specs=P("box", "grp", None, None),
        check_vma=False,
    )
```

```python
import functools

import jax
import jax.numpy as jnp
import numpy as np
from jax import lax
from jax.experimental import pallas as pl
from jax.experimental.pallas import tpu as pltpu
from jax.sharding import PartitionSpec as P

CAP = 2
LANES = 128
FACES, COARSE = 32, 8
ROWS = FACES + COARSE
OUTER = 4
PARTS = 4
BATCH = 4
VMEM_BYTES = 60 * 1024 * 1024
STEPS = ((-1, 0), (1, 0), (0, -1), (0, 1))
HIGHEST = lax.Precision.HIGHEST


def turn(x, shift, axis=1):
    shift = shift % x.shape[axis]
    return x if shift == 0 else pltpu.roll(x, shift, axis)


def lane_of(shape):
    return lax.broadcasted_iota(jnp.int32, shape, 1)


def groups_of(x):
    return [x[:, LANES * g : LANES * (g + 1)] for g in range(x.shape[1] // LANES)]


def faces(parts):
    lane = lane_of(parts[0].shape)
    m, a = lane % 32, lane // 32
    tile = jnp.zeros_like(parts[0])
    for g, part in enumerate(parts):
        tile = jnp.where(m == g, turn(part, g), tile)
        tile = jnp.where(m == 16 + g, turn(part, g - 15), tile)
    for k in range(4):
        here = a == k
        tile = jnp.where(here & (m >= 8) & (m < 16), turn(parts[0], 24 * k + 8), tile)
        tile = jnp.where(here & (m >= 24), turn(parts[-1], 24 * k - 72), tile)
    return tile


def spread(tile):
    lane = lane_of(tile.shape)
    m = lane % 32
    along_z = [jnp.where(m == 31, turn(tile, 15 - g), turn(tile, -g)) for g in range(8)]
    low = turn(tile, -8)
    high = turn(tile, 72)
    for a in range(1, 4):
        low = jnp.where(lane // 8 == a, turn(tile, -24 * a - 8), low)
        high = jnp.where((lane - 96) // 8 == a, turn(tile, 72 - 24 * a), high)
    return along_z, low, high


def swapped(tiles):
    m = lane_of(tiles[0].shape) % 32
    pick = jnp.where(m < 8, tiles[3], jnp.where(m < 16, tiles[1], jnp.where(m < 24, tiles[2], tiles[0])))
    return jnp.where(m < 16, turn(pick, -16), turn(pick, 16))


def around(parts, ghost, low_x, high_x, g):
    along_z, low_y, high_y = ghost
    x = parts[g]
    lane = lane_of(x.shape)
    m = lane % 32
    row = lax.broadcasted_iota(jnp.int32, x.shape, 0)
    cut = slice(LANES * g, LANES * (g + 1))
    minus_x = jnp.where(row == 0, low_x[:, cut], turn(x, 1, 0))
    plus_x = jnp.where(row == x.shape[0] - 1, high_x[:, cut], turn(x, -1, 0))
    if g == 0:
        minus_y = jnp.where(lane < 32, low_y, turn(x, 32))
    else:
        minus_y = turn(jnp.where(lane >= 96, parts[g - 1], x), 32)
    if g == len(parts) - 1:
        plus_y = jnp.where(lane >= 96, high_y, turn(x, -32))
    else:
        plus_y = turn(jnp.where(lane < 32, parts[g + 1], x), -32)
    minus_z = jnp.where(m == 0, along_z[g], turn(x, 1))
    plus_z = jnp.where(m == 31, along_z[g], turn(x, -1))
    return [minus_x, plus_x, minus_y, plus_y, minus_z, plus_z]


def half_sweep(colour, phi, rhs, beta, phi_tile, beta_tile, phi_x, beta_x):
    phis, rhss, betas = groups_of(phi), groups_of(rhs), groups_of(beta)
    phi_ghost, beta_ghost = spread(phi_tile), spread(beta_tile)
    out = []
    for g in range(len(phis)):
        b = betas[g]
        near_b = around(betas, beta_ghost, beta_x[0], beta_x[1], g)
        near_p = around(phis, phi_ghost, phi_x[0], phi_x[1], g)
        lane = lane_of(b.shape)
        row = lax.broadcasted_iota(jnp.int32, b.shape, 0)
        accum, total = 0.5 * rhss[g] / b, jnp.zeros_like(b)
        for other, value in zip(near_b, near_p):
            other = jnp.where(other > 0.0, other, b)
            ratio = other / (b + other)
            accum = accum + ratio * value
            total = total + ratio
        mine = (row + lane // 32 + lane) % 2 == colour
        out.append(jnp.where(mine, accum / total, phis[g]))
    return out


def face_colour(shape):
    lane = lane_of(shape)
    m, a = lane % 32, lane // 32
    row = lax.broadcasted_iota(jnp.int32, shape, 0)
    return (row + jnp.where((m & 8) == 0, a, m) + m // 16) % 2


def paired(x, axis):
    even = lax.broadcasted_iota(jnp.int32, x.shape, axis) % 2 == 0
    return jnp.where(even, turn(x, -1, axis), turn(x, 1, axis))


def mixed(colour, phi, beta):
    return jnp.where(face_colour(phi.shape) == colour, phi, paired(beta, 0))


def mixed_row(colour, first, phi, beta):
    lane = lane_of(phi.shape)
    return jnp.where((first + lane // 32 + lane) % 2 == colour, phi, paired(beta, 1))


def folded(x):
    lane = lane_of((COARSE, LANES))
    odd = jnp.where((lane & 8) == 0, lane // 32, lane) % 2 == 1
    return jnp.where(odd, x[COARSE:], x[:COARSE])


def unfolded(t):
    lane = lane_of(t.shape)
    along_z = (lane & 8) == 0
    odd = jnp.where(along_z, lane // 32, lane) % 2 == 1
    low = jnp.where(odd, jnp.where(along_z, turn(t, 32), turn(t, 1)), t)
    high = jnp.where(odd, t, jnp.where(along_z, turn(t, -32), turn(t, -1)))
    return low, high


def pack_kernel(count, pos, ref, phi, beta, coarse, pick, sent, up, down):
    q = pl.program_id(0)
    half = coarse.shape[1]

    @pl.when(q == 0)
    def _():
        wide = jnp.dot(
            coarse[...].reshape(count * half, coarse.shape[2]), pick[...],
            precision=HIGHEST, preferred_element_type=jnp.float32,
        )
        lane = lane_of((8, LANES))
        row = lax.broadcasted_iota(jnp.int32, (8, LANES), 0)
        meta = jnp.zeros((8, LANES), jnp.int32)
        for s in range(count):
            sent[s * ROWS + FACES : (s + 1) * ROWS, :] = folded(wide[s * half : (s + 1) * half])
            meta = jnp.where((lane == s) & (row == 0), pos[s], meta)
            meta = jnp.where((lane == s) & (row == 1), ref[s], meta)
        sent[count * ROWS :, :] = meta.astype(jnp.float32)

    for b in range(BATCH):
        tile = mixed(1, faces(groups_of(phi[b])), faces(groups_of(beta[b])))
        sent[pl.ds(pl.multiple_of((q * BATCH + b) * ROWS, 8), FACES), :] = tile
        down[b] = mixed_row(1, 0, phi[b, 0:1, :], beta[b, 0:1, :])
        up[b] = mixed_row(1, 1, phi[b, 31:32, :], beta[b, 31:32, :])


def exchange_kernel(n, slabs, sent, up, down, got, low, high, send, recv, x_send, x_recv, local):
    inner = n // OUTER
    me, slab = lax.axis_index("grp"), lax.axis_index("box")
    z, y = me // inner, me % inner

    def device(to):
        return {"grp": to}

    ends = [(z < OUTER - 1, "grp", me + inner), (z > 0, "grp", me - inner),
            (slab < slabs - 1, "box", slab + 1), (slab > 0, "box", slab - 1)]
    mates = [z * inner + (y + i) % inner for i in range(1, inner)]
    barrier = pltpu.get_barrier_semaphore()
    for there, axis, to in ends:
        @pl.when(there)
        def _(axis=axis, to=to):
            pl.semaphore_signal(barrier, inc=1, device_id={axis: to}, device_id_type=pl.DeviceIdType.MESH)
    for to in mates:
        pl.semaphore_signal(barrier, inc=1, device_id=device(to), device_id_type=pl.DeviceIdType.MESH)
    total = inner - 1
    for there, _, _ in ends:
        total = total + there.astype(jnp.int32)
    pl.semaphore_wait(barrier, total)

    rows = sent.shape[0]
    cuts = [rows * p // (8 * PARTS) * 8 for p in range(PARTS)] + [rows]

    def copy(src, block, lane, to, p):
        span = pl.ds(cuts[p], cuts[p + 1] - cuts[p])
        return pltpu.make_async_remote_copy(
            src_ref=sent.at[span] if src is None else got.at[src, span],
            dst_ref=got.at[block, span], send_sem=send.at[lane, block, p],
            recv_sem=recv.at[block, p], device_id=device(to), device_id_type=pl.DeviceIdType.MESH,
        )

    def beside(block, src, p):
        for i, to in enumerate(mates):
            copy(src, block, 2 + i, to, p).start()

    def along_x(src, dst, lane, to):
        return pltpu.make_async_remote_copy(
            src_ref=src, dst_ref=dst, send_sem=x_send.at[lane], recv_sem=x_recv.at[lane],
            device_id={"box": to}, device_id_type=pl.DeviceIdType.MESH,
        )

    for p in range(PARTS):
        pl.when(z < OUTER - 1)(lambda: copy(None, me, 0, me + inner, p).start())
        pl.when(z > 0)(lambda: copy(None, me, 1, me - inner, p).start())
        beside(me, None, p)
    pl.when(slab < slabs - 1)(lambda: along_x(up, low, 0, slab + 1).start())
    pl.when(slab > 0)(lambda: along_x(down, high, 1, slab - 1).start())
    own = pltpu.make_async_copy(sent, got.at[me], local)
    own.start()
    for s in range(1, OUTER):
        for p in range(PARTS):
            @pl.when(z >= s)
            def _(s=s, p=p):
                block = me - s * inner
                copy(block, block, 0, block, p).wait_recv()
                pl.when(z < OUTER - 1)(lambda: copy(block, block, 0, me + inner, p).start())
                beside(block, block, p)

            @pl.when(z + s < OUTER)
            def _(s=s, p=p):
                block = me + s * inner
                copy(block, block, 1, block, p).wait_recv()
                pl.when(z > 0)(lambda: copy(block, block, 1, me - inner, p).start())
                beside(block, block, p)
    for level in range(OUTER):
        for i, to in enumerate(mates):
            block = level * inner + (y + i + 1) % inner
            for p in range(PARTS):
                copy(block, block, 2, to, p).wait_recv()
    own.wait()
    pl.when(slab > 0)(lambda: along_x(up, low, 0, slab - 1).wait_recv())
    pl.when(slab < slabs - 1)(lambda: along_x(down, high, 1, slab + 1).wait_recv())
    for level in range(OUTER):
        block = level * inner + y
        for p in range(PARTS):
            up_link, down_link = (z < OUTER - 1) & (level <= z), (z > 0) & (level >= z)
            pl.when(up_link)(lambda: copy(None, block, 0, me + inner, p).wait_send())
            pl.when(down_link)(lambda: copy(None, block, 1, me - inner, p).wait_send())
            for i, to in enumerate(mates):
                copy(None, block, 2 + i, to, p).wait_send()
    pl.when(slab < slabs - 1)(lambda: along_x(up, low, 0, slab + 1).wait_send())
    pl.when(slab > 0)(lambda: along_x(down, high, 1, slab - 1).wait_send())


def exchanged(number, sent, up, down):
    n, slabs = lax.axis_size("grp"), lax.axis_size("box")
    anywhere = pl.BlockSpec(memory_space=pl.ANY)
    return pl.pallas_call(
        functools.partial(exchange_kernel, n, slabs),
        out_shape=(struct(n, *sent.shape), struct(*up.shape), struct(*down.shape)),
        in_specs=[anywhere] * 3,
        out_specs=(anywhere,) * 3,
        scratch_shapes=[
            pltpu.SemaphoreType.DMA((1 + n // OUTER, n, PARTS)),
            pltpu.SemaphoreType.DMA((n, PARTS)),
            pltpu.SemaphoreType.DMA((2,)), pltpu.SemaphoreType.DMA((2,)), pltpu.SemaphoreType.DMA,
        ],
        compiler_params=pltpu.CompilerParams(
            collective_id=number, has_side_effects=True, vmem_limit_bytes=VMEM_BYTES
        ),
        name="exchange",
    )(sent, up, down)


def halo_rows(low, high):
    slab, slabs = lax.axis_index("box"), lax.axis_size("box")
    below = jnp.where(slab > 0, low, 0.0)
    above = jnp.where(slab < slabs - 1, high, 0.0)
    return (below, above), (paired(below, 1), paired(above, 1))


def first_kernel(
    count, slots, meta, pos, own, phi, rhs, beta, got, low, high,
    out, tile, up, down, coarse_tile, near, source, holder, filled, wide,
):
    q = pl.program_id(0)
    groups = slots // count

    def refined_at(p):
        return meta[(lax.div(p, count) * 2 + 1) * count + lax.rem(p, count)] > 0

    def rows(s, first, length):
        start = pl.multiple_of(lax.rem(s, count) * ROWS + first, 8)
        return got[lax.div(s, count), pl.ds(start, length), :]

    @pl.when(q == 0)
    def _():
        def place(s, carry):
            holder[meta[lax.div(s, count) * 2 * count + lax.rem(s, count)]] = s
            return carry

        lax.fori_loop(0, slots, place, 0)

        def clear(s, carry):
            source[s] = -1
            return carry

        lax.fori_loop(0, groups * CAP, clear, 0)

        def empty(s, carry):
            filled[s] = 0
            return carry

        lax.fori_loop(0, groups, empty, 0)

        def give(s, carry):
            to = own[s]
            rank = filled[to]
            filled[to] = rank + 1
            live = refined_at(pos[s])
            source[to * CAP + rank] = jnp.where(live, s, -1)
            return carry

        lax.fori_loop(0, count, give, 0)

    here = pos[q]
    row, col = lax.div(here, count), lax.rem(here, count)
    fine_tiles, under = [], []
    for k, (dy, dz) in enumerate(STEPS):
        y, z = row + dy, col + dz
        inside = (y >= 0) & (y < groups) & (z >= 0) & (z < count)
        spot = jnp.where(inside, y * count + z, 0)
        fine = inside & refined_at(spot)
        slot = holder[spot]
        near[q * 4 + k] = jnp.where(fine, slot, -1)
        fine_tiles.append(jnp.where(fine, rows(slot, 0, FACES), 0.0))
        under.append(jnp.where(inside & jnp.logical_not(fine), rows(spot, FACES, COARSE), 0.0))
    for i, narrow in enumerate(unfolded(swapped(under))):
        for odd in range(2):
            wide[pl.ds(2 * COARSE * i + odd, COARSE, stride=2), :] = narrow
    coarse_ghost = wide[...]
    coarse_tile[0] = coarse_ghost
    ghost = swapped(fine_tiles)
    phi_x, beta_x = halo_rows(low[0], high[0])
    parts = half_sweep(
        0, phi[0], rhs[0], beta[0], ghost + coarse_ghost, paired(ghost, 0), phi_x, beta_x
    )
    for g, part in enumerate(parts):
        cut = slice(LANES * g, LANES * (g + 1))
        out[0, :, cut] = part
        down[0, :, cut] = mixed_row(0, 0, part[0:1], beta[0, 0:1, cut])
        up[0, :, cut] = mixed_row(0, 1, part[31:32], beta[0, 31:32, cut])
    tile[...] = mixed(0, faces(parts), faces(groups_of(beta[0])))


def deliver_kernel(
    n, near, source, phi, rhs, beta, got, low, high, coarse_tile, moved, ready, send, recv, local
):
    me = lax.axis_index("grp")
    barrier = pltpu.get_barrier_semaphore()
    for i in range(1, n):
        pl.semaphore_signal(
            barrier, inc=1, device_id={"grp": (me + i) % n}, device_id_type=pl.DeviceIdType.MESH
        )
    pl.semaphore_wait(barrier, n - 1)
    side, place = me // (n // 2), me % (n // 2)

    def copy(mine, theirs, to):
        return pltpu.make_async_remote_copy(
            src_ref=ready.at[mine], dst_ref=moved.at[theirs], send_sem=send.at[mine],
            recv_sem=recv.at[theirs], device_id={"grp": to}, device_id_type=pl.DeviceIdType.MESH,
        )

    def solve(mine):
        q = source[mine]
        box = jnp.maximum(q, 0)
        tiles = []
        for k in range(4):
            slot = near[box * 4 + k]
            tiles.append(jnp.where(slot >= 0, got[jnp.maximum(slot, 0)], 0.0))
        ghost = swapped(tiles)
        phi_x, beta_x = halo_rows(low[box], high[box])
        parts = half_sweep(
            1, phi[box], rhs[box], beta[box], ghost + coarse_tile[box], paired(ghost, 0),
            phi_x, beta_x,
        )
        for g, part in enumerate(parts):
            ready[mine, :, LANES * g : LANES * (g + 1)] = jnp.where(q >= 0, part, 0.0)

    def one(t, carry):
        i, c = t // CAP, t % CAP
        far = (1 - side) * (n // 2) + (place + i) % (n // 2)
        close = side * (n // 2) + (place + i + 1) % (n // 2)
        to = jnp.where(i < n // 2, far, close)
        mine = to * CAP + c
        solve(mine)
        pl.when(i < n - 1)(lambda: copy(mine, me * CAP + c, to).start())
        return carry

    lax.fori_loop(0, n * CAP, one, 0)
    own = [
        pltpu.make_async_copy(ready.at[me * CAP + c], moved.at[me * CAP + c], local.at[c])
        for c in range(CAP)
    ]
    for each in own:
        each.start()
    for i in range(1, n):
        other = (me + i) % n
        for c in range(CAP):
            copy(other * CAP + c, other * CAP + c, other).wait()
    for each in own:
        each.wait()


def coarse_pick(half):
    lane = np.arange(LANES)
    m, a = lane % 32, lane // 32
    j = m % 8
    y = np.select([m < 8, m < 16, m < 24], [4 * j + a, 0 * a, 4 * j + a], 2 * half - 1 + 0 * a)
    z = np.select([m < 8, m < 16, m < 24], [0 * a, 8 * a + j, 2 * half - 1 + 0 * a], 8 * a + j)
    cell = (y // 2) * half + z // 2
    return (np.arange(half * half)[:, None] == cell[None, :]).astype(np.float32)


def struct(*shape, dtype=jnp.float32):
    return jax.ShapeDtypeStruct(shape, dtype)


def shards(old_phi, old_rhs, old_beta, coarse_field, old_pos, refined, new_owner):
    phi, rhs, beta, coarse = old_phi[0], old_rhs[0], old_beta[0], coarse_field[0]
    count, edge, area = phi.shape
    groups = lax.axis_size("grp")
    slots = count * groups
    owner = new_owner[:, 0]
    smem = pl.BlockSpec(memory_space=pltpu.SMEM)
    params = pltpu.CompilerParams(vmem_limit_bytes=VMEM_BYTES)
    def own(*shape):
        return pl.BlockSpec((1,) + shape, lambda q, *_: (q, 0, 0))

    def batch(*shape):
        return pl.BlockSpec((BATCH,) + shape, lambda q, *_: (q, 0, 0))

    def full(*shape):
        return pl.BlockSpec(shape, lambda q, *_: (0, 0, 0))

    box = own(edge, area)
    sent, up, down = pl.pallas_call(
        functools.partial(pack_kernel, count),
        out_shape=(
            struct(count * ROWS + 8, LANES), struct(count, 1, area), struct(count, 1, area)
        ),
        grid_spec=pltpu.PrefetchScalarGridSpec(
            num_scalar_prefetch=2,
            grid=(count // BATCH,),
            in_specs=[
                batch(edge, area), batch(edge, area), full(*coarse.shape), pl.BlockSpec((area // 4, LANES), lambda q, *_: (0, 0))
            ],
            out_specs=[
                pl.BlockSpec((count * ROWS + 8, LANES), lambda q, *_: (0, 0)), batch(1, area),
                batch(1, area),
            ],
        ),
        compiler_params=params,
        name="pack",
    )(old_pos, refined, phi, beta, coarse, jnp.asarray(coarse_pick(edge // 2)))
    got, low, high = exchanged(0, sent, up, down)
    meta = got[:, count * ROWS : count * ROWS + 2, :count].astype(jnp.int32).reshape(2 * slots)

    middle, tile, up2, down2, coarse_tile, near, source = pl.pallas_call(
        functools.partial(first_kernel, count, slots),
        out_shape=(
            struct(count, edge, area), struct(count * edge, LANES), struct(count, 1, area),
            struct(count, 1, area), struct(count, edge, LANES),
            struct(count * 4, dtype=jnp.int32), struct(groups * CAP, dtype=jnp.int32),
        ),
        grid_spec=pltpu.PrefetchScalarGridSpec(
            num_scalar_prefetch=3,
            grid=(count,),
            in_specs=[box, box, box, full(groups, count * ROWS + 8, LANES), own(1, area), own(1, area)],
            out_specs=[
                box, pl.BlockSpec((edge, LANES), lambda q, *_: (q, 0)), own(1, area), own(1, area),
                own(edge, LANES), smem, smem,
            ],
            scratch_shapes=[
                pltpu.SMEM((slots,), jnp.int32), pltpu.SMEM((groups,), jnp.int32),
                pltpu.VMEM((edge, LANES), jnp.float32),
            ],
        ),
        compiler_params=params,
        name="colour0",
    )(meta, old_pos, owner, phi, rhs, beta, got, low, high)
    got2, low2, high2 = exchanged(1, tile, up2, down2)

    vmem = pl.BlockSpec(memory_space=pltpu.VMEM)
    moved = pl.pallas_call(
        functools.partial(deliver_kernel, groups),
        out_shape=struct(groups * CAP, edge, area),
        in_specs=[smem, smem] + [vmem] * 7,
        out_specs=pl.BlockSpec(memory_space=pl.ANY),
        scratch_shapes=[
            pltpu.VMEM((groups * CAP, edge, area), jnp.float32),
            pltpu.SemaphoreType.DMA((groups * CAP,)), pltpu.SemaphoreType.DMA((groups * CAP,)),
            pltpu.SemaphoreType.DMA((CAP,)),
        ],
        compiler_params=pltpu.CompilerParams(
            collective_id=2, has_side_effects=True, vmem_limit_bytes=VMEM_BYTES
        ),
        name="deliver",
    )(near, source, middle, rhs, beta, got2.reshape(slots, edge, LANES), low2, high2, coarse_tile)
    return moved[None]


def solution(mesh):
    return jax.shard_map(
        shards,
        mesh=mesh,
        in_specs=(
            P("box", "grp", None, None),
            P("box", "grp", None, None),
            P("box", "grp", None, None),
            P("box", "grp", None, None),
            P("grp"),
            P("grp"),
            P("grp", None),
        ),
        out_specs=P("box", "grp", None, None),
        check_vma=False,
    )
```

```python
import functools

import jax
import jax.numpy as jnp
import numpy as np
from jax import lax
from jax.experimental import pallas as pl
from jax.experimental.pallas import tpu as pltpu
from jax.sharding import PartitionSpec as P

CAP = 2
LANES = 128
FACES, COARSE = 32, 8
ROWS = FACES + COARSE
OUTER = 4
PARTS = 4
BATCH = 4
VMEM_BYTES = 60 * 1024 * 1024
STEPS = ((-1, 0), (1, 0), (0, -1), (0, 1))
HIGHEST = lax.Precision.HIGHEST


def turn(x, shift, axis=1):
    shift = shift % x.shape[axis]
    return x if shift == 0 else pltpu.roll(x, shift, axis)


def lane_of(shape):
    return lax.broadcasted_iota(jnp.int32, shape, 1)


def groups_of(x):
    return [x[:, LANES * g : LANES * (g + 1)] for g in range(x.shape[1] // LANES)]


def faces(parts):
    lane = lane_of(parts[0].shape)
    m, a = lane % 32, lane // 32
    tile = jnp.zeros_like(parts[0])
    for g, part in enumerate(parts):
        tile = jnp.where(m == g, turn(part, g), tile)
        tile = jnp.where(m == 16 + g, turn(part, g - 15), tile)
    for k in range(4):
        here = a == k
        tile = jnp.where(here & (m >= 8) & (m < 16), turn(parts[0], 24 * k + 8), tile)
        tile = jnp.where(here & (m >= 24), turn(parts[-1], 24 * k - 72), tile)
    return tile


def spread(tile):
    lane = lane_of(tile.shape)
    m = lane % 32
    along_z = [jnp.where(m == 31, turn(tile, 15 - g), turn(tile, -g)) for g in range(8)]
    low = turn(tile, -8)
    high = turn(tile, 72)
    for a in range(1, 4):
        low = jnp.where(lane // 8 == a, turn(tile, -24 * a - 8), low)
        high = jnp.where((lane - 96) // 8 == a, turn(tile, 72 - 24 * a), high)
    return along_z, low, high


def swapped(tiles):
    m = lane_of(tiles[0].shape) % 32
    pick = jnp.where(m < 8, tiles[3], jnp.where(m < 16, tiles[1], jnp.where(m < 24, tiles[2], tiles[0])))
    return jnp.where(m < 16, turn(pick, -16), turn(pick, 16))


def around(parts, ghost, low_x, high_x, g):
    along_z, low_y, high_y = ghost
    x = parts[g]
    lane = lane_of(x.shape)
    m = lane % 32
    row = lax.broadcasted_iota(jnp.int32, x.shape, 0)
    cut = slice(LANES * g, LANES * (g + 1))
    minus_x = jnp.where(row == 0, low_x[:, cut], turn(x, 1, 0))
    plus_x = jnp.where(row == x.shape[0] - 1, high_x[:, cut], turn(x, -1, 0))
    if g == 0:
        minus_y = jnp.where(lane < 32, low_y, turn(x, 32))
    else:
        minus_y = turn(jnp.where(lane >= 96, parts[g - 1], x), 32)
    if g == len(parts) - 1:
        plus_y = jnp.where(lane >= 96, high_y, turn(x, -32))
    else:
        plus_y = turn(jnp.where(lane < 32, parts[g + 1], x), -32)
    minus_z = jnp.where(m == 0, along_z[g], turn(x, 1))
    plus_z = jnp.where(m == 31, along_z[g], turn(x, -1))
    return [minus_x, plus_x, minus_y, plus_y, minus_z, plus_z]


def half_sweep(colour, phi, rhs, beta, phi_tile, beta_tile, phi_x, beta_x):
    phis, rhss, betas = groups_of(phi), groups_of(rhs), groups_of(beta)
    phi_ghost, beta_ghost = spread(phi_tile), spread(beta_tile)
    out = []
    for g in range(len(phis)):
        b = betas[g]
        near_b = around(betas, beta_ghost, beta_x[0], beta_x[1], g)
        near_p = around(phis, phi_ghost, phi_x[0], phi_x[1], g)
        lane = lane_of(b.shape)
        row = lax.broadcasted_iota(jnp.int32, b.shape, 0)
        accum, total = 0.5 * rhss[g] / b, jnp.zeros_like(b)
        for other, value in zip(near_b, near_p):
            other = jnp.where(other > 0.0, other, b)
            ratio = other / (b + other)
            accum = accum + ratio * value
            total = total + ratio
        mine = (row + lane // 32 + lane) % 2 == colour
        out.append(jnp.where(mine, accum / total, phis[g]))
    return out


def face_colour(shape):
    lane = lane_of(shape)
    m, a = lane % 32, lane // 32
    row = lax.broadcasted_iota(jnp.int32, shape, 0)
    return (row + jnp.where((m & 8) == 0, a, m) + m // 16) % 2


def paired(x, axis):
    even = lax.broadcasted_iota(jnp.int32, x.shape, axis) % 2 == 0
    return jnp.where(even, turn(x, -1, axis), turn(x, 1, axis))


def mixed(colour, phi, beta):
    return jnp.where(face_colour(phi.shape) == colour, phi, paired(beta, 0))


def mixed_row(colour, first, phi, beta):
    lane = lane_of(phi.shape)
    return jnp.where((first + lane // 32 + lane) % 2 == colour, phi, paired(beta, 1))


def folded(x):
    lane = lane_of((COARSE, LANES))
    odd = jnp.where((lane & 8) == 0, lane // 32, lane) % 2 == 1
    return jnp.where(odd, x[COARSE:], x[:COARSE])


def unfolded(t):
    lane = lane_of(t.shape)
    along_z = (lane & 8) == 0
    odd = jnp.where(along_z, lane // 32, lane) % 2 == 1
    low = jnp.where(odd, jnp.where(along_z, turn(t, 32), turn(t, 1)), t)
    high = jnp.where(odd, t, jnp.where(along_z, turn(t, -32), turn(t, -1)))
    return low, high


def pack_kernel(count, pos, ref, phi, beta, coarse, pick, sent, up, down):
    q = pl.program_id(0)
    half = coarse.shape[1]

    @pl.when(q == 0)
    def _():
        wide = jnp.dot(
            coarse[...].reshape(count * half, coarse.shape[2]), pick[...],
            precision=HIGHEST, preferred_element_type=jnp.float32,
        )
        lane = lane_of((8, LANES))
        row = lax.broadcasted_iota(jnp.int32, (8, LANES), 0)
        meta = jnp.zeros((8, LANES), jnp.int32)
        for s in range(count):
            sent[s * ROWS + FACES : (s + 1) * ROWS, :] = folded(wide[s * half : (s + 1) * half])
            meta = jnp.where((lane == s) & (row == 0), pos[s], meta)
            meta = jnp.where((lane == s) & (row == 1), ref[s], meta)
        sent[count * ROWS :, :] = meta.astype(jnp.float32)

    for b in range(BATCH):
        tile = mixed(1, faces(groups_of(phi[b])), faces(groups_of(beta[b])))
        sent[pl.ds(pl.multiple_of((q * BATCH + b) * ROWS, 8), FACES), :] = tile
        down[b] = mixed_row(1, 0, phi[b, 0:1, :], beta[b, 0:1, :])
        up[b] = mixed_row(1, 1, phi[b, 31:32, :], beta[b, 31:32, :])


def exchange_kernel(n, slabs, sent, up, down, got, low, high, send, recv, x_send, x_recv, local):
    inner = n // OUTER
    me, slab = lax.axis_index("grp"), lax.axis_index("box")
    z, y = me // inner, me % inner

    def device(to):
        return {"grp": to}

    ends = [(z < OUTER - 1, "grp", me + inner), (z > 0, "grp", me - inner),
            (slab < slabs - 1, "box", slab + 1), (slab > 0, "box", slab - 1)]
    mates = [z * inner + (y + i) % inner for i in range(1, inner)]
    barrier = pltpu.get_barrier_semaphore()
    for there, axis, to in ends:
        @pl.when(there)
        def _(axis=axis, to=to):
            pl.semaphore_signal(barrier, inc=1, device_id={axis: to}, device_id_type=pl.DeviceIdType.MESH)
    for to in mates:
        pl.semaphore_signal(barrier, inc=1, device_id=device(to), device_id_type=pl.DeviceIdType.MESH)
    total = inner - 1
    for there, _, _ in ends:
        total = total + there.astype(jnp.int32)
    pl.semaphore_wait(barrier, total)

    rows = sent.shape[0]
    cuts = [rows * p // (8 * PARTS) * 8 for p in range(PARTS)] + [rows]

    def copy(src, block, lane, to, p):
        span = pl.ds(cuts[p], cuts[p + 1] - cuts[p])
        return pltpu.make_async_remote_copy(
            src_ref=sent.at[span] if src is None else got.at[src, span],
            dst_ref=got.at[block, span], send_sem=send.at[lane, block, p],
            recv_sem=recv.at[block, p], device_id=device(to), device_id_type=pl.DeviceIdType.MESH,
        )

    def beside(block, src, p):
        for i, to in enumerate(mates):
            copy(src, block, 2 + i, to, p).start()

    def along_x(src, dst, lane, to):
        return pltpu.make_async_remote_copy(
            src_ref=src, dst_ref=dst, send_sem=x_send.at[lane], recv_sem=x_recv.at[lane],
            device_id={"box": to}, device_id_type=pl.DeviceIdType.MESH,
        )

    for p in range(PARTS):
        pl.when(z < OUTER - 1)(lambda: copy(None, me, 0, me + inner, p).start())
        pl.when(z > 0)(lambda: copy(None, me, 1, me - inner, p).start())
        beside(me, None, p)
    pl.when(slab < slabs - 1)(lambda: along_x(up, low, 0, slab + 1).start())
    pl.when(slab > 0)(lambda: along_x(down, high, 1, slab - 1).start())
    own = pltpu.make_async_copy(sent, got.at[me], local)
    own.start()
    for s in range(1, OUTER):
        for p in range(PARTS):
            @pl.when(z >= s)
            def _(s=s, p=p):
                block = me - s * inner
                copy(block, block, 0, block, p).wait_recv()
                pl.when(z < OUTER - 1)(lambda: copy(block, block, 0, me + inner, p).start())
                beside(block, block, p)

            @pl.when(z + s < OUTER)
            def _(s=s, p=p):
                block = me + s * inner
                copy(block, block, 1, block, p).wait_recv()
                pl.when(z > 0)(lambda: copy(block, block, 1, me - inner, p).start())
                beside(block, block, p)
    for level in range(OUTER):
        for i, to in enumerate(mates):
            block = level * inner + (y + i + 1) % inner
            for p in range(PARTS):
                copy(block, block, 2, to, p).wait_recv()
    own.wait()
    pl.when(slab > 0)(lambda: along_x(up, low, 0, slab - 1).wait_recv())
    pl.when(slab < slabs - 1)(lambda: along_x(down, high, 1, slab + 1).wait_recv())
    for level in range(OUTER):
        block = level * inner + y
        for p in range(PARTS):
            up_link, down_link = (z < OUTER - 1) & (level <= z), (z > 0) & (level >= z)
            pl.when(up_link)(lambda: copy(None, block, 0, me + inner, p).wait_send())
            pl.when(down_link)(lambda: copy(None, block, 1, me - inner, p).wait_send())
            for i, to in enumerate(mates):
                copy(None, block, 2 + i, to, p).wait_send()
    pl.when(slab < slabs - 1)(lambda: along_x(up, low, 0, slab + 1).wait_send())
    pl.when(slab > 0)(lambda: along_x(down, high, 1, slab - 1).wait_send())


def exchanged(number, sent, up, down):
    n, slabs = lax.axis_size("grp"), lax.axis_size("box")
    anywhere = pl.BlockSpec(memory_space=pl.ANY)
    return pl.pallas_call(
        functools.partial(exchange_kernel, n, slabs),
        out_shape=(struct(n, *sent.shape), struct(*up.shape), struct(*down.shape)),
        in_specs=[anywhere] * 3,
        out_specs=(anywhere,) * 3,
        scratch_shapes=[
            pltpu.SemaphoreType.DMA((1 + n // OUTER, n, PARTS)),
            pltpu.SemaphoreType.DMA((n, PARTS)),
            pltpu.SemaphoreType.DMA((2,)), pltpu.SemaphoreType.DMA((2,)), pltpu.SemaphoreType.DMA,
        ],
        compiler_params=pltpu.CompilerParams(
            collective_id=number, has_side_effects=True, vmem_limit_bytes=VMEM_BYTES
        ),
        name="exchange",
    )(sent, up, down)


def halo_rows(low, high):
    slab, slabs = lax.axis_index("box"), lax.axis_size("box")
    below = jnp.where(slab > 0, low, 0.0)
    above = jnp.where(slab < slabs - 1, high, 0.0)
    return (below, above), (paired(below, 1), paired(above, 1))


def first_kernel(
    count, slots, meta, pos, own, phi, rhs, beta, got, low, high,
    out, tile, up, down, coarse_tile, near, source, holder, filled, wide,
):
    q = pl.program_id(0)
    groups = slots // count

    def refined_at(p):
        return meta[(lax.div(p, count) * 2 + 1) * count + lax.rem(p, count)] > 0

    def rows(s, first, length):
        start = pl.multiple_of(lax.rem(s, count) * ROWS + first, 8)
        return got[lax.div(s, count), pl.ds(start, length), :]

    @pl.when(q == 0)
    def _():
        def place(s, carry):
            holder[meta[lax.div(s, count) * 2 * count + lax.rem(s, count)]] = s
            return carry

        lax.fori_loop(0, slots, place, 0)

        def clear(s, carry):
            source[s] = -1
            return carry

        lax.fori_loop(0, groups * CAP, clear, 0)

        def empty(s, carry):
            filled[s] = 0
            return carry

        lax.fori_loop(0, groups, empty, 0)

        def give(s, carry):
            to = own[s]
            rank = filled[to]
            filled[to] = rank + 1
            live = refined_at(pos[s])
            source[to * CAP + rank] = jnp.where(live, s, -1)
            return carry

        lax.fori_loop(0, count, give, 0)

    def one(b, carry):
        box = q * BATCH + b
        here = pos[box]
        row, col = lax.div(here, count), lax.rem(here, count)
        fine_tiles, under = [], []
        for k, (dy, dz) in enumerate(STEPS):
            y, z = row + dy, col + dz
            inside = (y >= 0) & (y < groups) & (z >= 0) & (z < count)
            spot = jnp.where(inside, y * count + z, 0)
            fine = inside & refined_at(spot)
            slot = holder[spot]
            near[box * 4 + k] = jnp.where(fine, slot, -1)
            fine_tiles.append(jnp.where(fine, rows(slot, 0, FACES), 0.0))
            under.append(jnp.where(inside & jnp.logical_not(fine), rows(spot, FACES, COARSE), 0.0))
        for i, narrow in enumerate(unfolded(swapped(under))):
            for odd in range(2):
                wide[pl.ds(2 * COARSE * i + odd, COARSE, stride=2), :] = narrow
        coarse_ghost = wide[...]
        coarse_tile[b] = coarse_ghost
        ghost = swapped(fine_tiles)
        phi_x, beta_x = halo_rows(low[b], high[b])
        parts = half_sweep(
            0, phi[b], rhs[b], beta[b], ghost + coarse_ghost, paired(ghost, 0), phi_x, beta_x
        )
        for g, part in enumerate(parts):
            cut = slice(LANES * g, LANES * (g + 1))
            out[b, :, cut] = part
            down[b, :, cut] = mixed_row(0, 0, part[0:1], beta[b, 0:1, cut])
            up[b, :, cut] = mixed_row(0, 1, part[31:32], beta[b, 31:32, cut])
        tile[pl.ds(pl.multiple_of(b * FACES, 8), FACES), :] = mixed(
            0, faces(parts), faces(groups_of(beta[b]))
        )
        return carry

    lax.fori_loop(0, BATCH, one, 0)


def deliver_kernel(
    n, near, source, phi, rhs, beta, got, low, high, coarse_tile, moved, ready, send, recv, local
):
    me = lax.axis_index("grp")
    barrier = pltpu.get_barrier_semaphore()
    for i in range(1, n):
        pl.semaphore_signal(
            barrier, inc=1, device_id={"grp": (me + i) % n}, device_id_type=pl.DeviceIdType.MESH
        )
    pl.semaphore_wait(barrier, n - 1)
    side, place = me // (n // 2), me % (n // 2)

    def copy(mine, theirs, to):
        return pltpu.make_async_remote_copy(
            src_ref=ready.at[mine], dst_ref=moved.at[theirs], send_sem=send.at[mine],
            recv_sem=recv.at[theirs], device_id={"grp": to}, device_id_type=pl.DeviceIdType.MESH,
        )

    def solve(mine):
        q = source[mine]
        box = jnp.maximum(q, 0)
        tiles = []
        for k in range(4):
            slot = near[box * 4 + k]
            tiles.append(jnp.where(slot >= 0, got[jnp.maximum(slot, 0)], 0.0))
        ghost = swapped(tiles)
        phi_x, beta_x = halo_rows(low[box], high[box])
        parts = half_sweep(
            1, phi[box], rhs[box], beta[box], ghost + coarse_tile[box], paired(ghost, 0),
            phi_x, beta_x,
        )
        for g, part in enumerate(parts):
            ready[mine, :, LANES * g : LANES * (g + 1)] = jnp.where(q >= 0, part, 0.0)

    def one(t, carry):
        i, c = t // CAP, t % CAP
        far = (1 - side) * (n // 2) + (place + i) % (n // 2)
        close = side * (n // 2) + (place + i + 1) % (n // 2)
        to = jnp.where(i < n // 2, far, close)
        mine = to * CAP + c
        solve(mine)
        pl.when(i < n - 1)(lambda: copy(mine, me * CAP + c, to).start())
        return carry

    lax.fori_loop(0, n * CAP, one, 0)
    own = [
        pltpu.make_async_copy(ready.at[me * CAP + c], moved.at[me * CAP + c], local.at[c])
        for c in range(CAP)
    ]
    for each in own:
        each.start()
    for i in range(1, n):
        other = (me + i) % n
        for c in range(CAP):
            copy(other * CAP + c, other * CAP + c, other).wait()
    for each in own:
        each.wait()


def coarse_pick(half):
    lane = np.arange(LANES)
    m, a = lane % 32, lane // 32
    j = m % 8
    y = np.select([m < 8, m < 16, m < 24], [4 * j + a, 0 * a, 4 * j + a], 2 * half - 1 + 0 * a)
    z = np.select([m < 8, m < 16, m < 24], [0 * a, 8 * a + j, 2 * half - 1 + 0 * a], 8 * a + j)
    cell = (y // 2) * half + z // 2
    return (np.arange(half * half)[:, None] == cell[None, :]).astype(np.float32)


def struct(*shape, dtype=jnp.float32):
    return jax.ShapeDtypeStruct(shape, dtype)


def shards(old_phi, old_rhs, old_beta, coarse_field, old_pos, refined, new_owner):
    phi, rhs, beta, coarse = old_phi[0], old_rhs[0], old_beta[0], coarse_field[0]
    count, edge, area = phi.shape
    groups = lax.axis_size("grp")
    slots = count * groups
    owner = new_owner[:, 0]
    smem = pl.BlockSpec(memory_space=pltpu.SMEM)
    params = pltpu.CompilerParams(vmem_limit_bytes=VMEM_BYTES)
    def own(*shape):
        return pl.BlockSpec((1,) + shape, lambda q, *_: (q, 0, 0))

    def batch(*shape):
        return pl.BlockSpec((BATCH,) + shape, lambda q, *_: (q, 0, 0))

    def full(*shape):
        return pl.BlockSpec(shape, lambda q, *_: (0, 0, 0))

    sent, up, down = pl.pallas_call(
        functools.partial(pack_kernel, count),
        out_shape=(
            struct(count * ROWS + 8, LANES), struct(count, 1, area), struct(count, 1, area)
        ),
        grid_spec=pltpu.PrefetchScalarGridSpec(
            num_scalar_prefetch=2,
            grid=(count // BATCH,),
            in_specs=[
                batch(edge, area), batch(edge, area), full(*coarse.shape), pl.BlockSpec((area // 4, LANES), lambda q, *_: (0, 0))
            ],
            out_specs=[
                pl.BlockSpec((count * ROWS + 8, LANES), lambda q, *_: (0, 0)), batch(1, area),
                batch(1, area),
            ],
        ),
        compiler_params=params,
        name="pack",
    )(old_pos, refined, phi, beta, coarse, jnp.asarray(coarse_pick(edge // 2)))
    got, low, high = exchanged(0, sent, up, down)
    meta = got[:, count * ROWS : count * ROWS + 2, :count].astype(jnp.int32).reshape(2 * slots)

    middle, tile, up2, down2, coarse_tile, near, source = pl.pallas_call(
        functools.partial(first_kernel, count, slots),
        out_shape=(
            struct(count, edge, area), struct(count * edge, LANES), struct(count, 1, area),
            struct(count, 1, area), struct(count, edge, LANES),
            struct(count * 4, dtype=jnp.int32), struct(groups * CAP, dtype=jnp.int32),
        ),
        grid_spec=pltpu.PrefetchScalarGridSpec(
            num_scalar_prefetch=3,
            grid=(count // BATCH,),
            in_specs=[batch(edge, area)] * 3 + [full(groups, count * ROWS + 8, LANES), batch(1, area), batch(1, area)],
            out_specs=[
                batch(edge, area), pl.BlockSpec((BATCH * edge, LANES), lambda q, *_: (q, 0)), batch(1, area), batch(1, area),
                batch(edge, LANES), smem, smem,
            ],
            scratch_shapes=[
                pltpu.SMEM((slots,), jnp.int32), pltpu.SMEM((groups,), jnp.int32),
                pltpu.VMEM((edge, LANES), jnp.float32),
            ],
        ),
        compiler_params=params,
        name="colour0",
    )(meta, old_pos, owner, phi, rhs, beta, got, low, high)
    got2, low2, high2 = exchanged(1, tile, up2, down2)

    vmem = pl.BlockSpec(memory_space=pltpu.VMEM)
    moved = pl.pallas_call(
        functools.partial(deliver_kernel, groups),
        out_shape=struct(groups * CAP, edge, area),
        in_specs=[smem, smem] + [vmem] * 7,
        out_specs=pl.BlockSpec(memory_space=pl.ANY),
        scratch_shapes=[
            pltpu.VMEM((groups * CAP, edge, area), jnp.float32),
            pltpu.SemaphoreType.DMA((groups * CAP,)), pltpu.SemaphoreType.DMA((groups * CAP,)),
            pltpu.SemaphoreType.DMA((CAP,)),
        ],
        compiler_params=pltpu.CompilerParams(
            collective_id=2, has_side_effects=True, vmem_limit_bytes=VMEM_BYTES
        ),
        name="deliver",
    )(near, source, middle, rhs, beta, got2.reshape(slots, edge, LANES), low2, high2, coarse_tile)
    return moved[None]


def solution(mesh):
    return jax.shard_map(
        shards,
        mesh=mesh,
        in_specs=(
            P("box", "grp", None, None),
            P("box", "grp", None, None),
            P("box", "grp", None, None),
            P("box", "grp", None, None),
            P("grp"),
            P("grp"),
            P("grp", None),
        ),
        out_specs=P("box", "grp", None, None),
        check_vma=False,
    )
```
